512 devices in a mesh: fsdp: 16 (over z_lo, core), tensor: 4 (over y), replica: 8 (over x, z_hi).
Axes of the slice: x: 4, y: 4, z: 16 (z_hi: 2, z_lo: 8; z = z_hi * 8 + z_lo), core: 2. Of those that a mesh axis runs over, the one named last changes fastest.
Arguments:
- hidden: bfloat16 [4, 128, 8192], P(None, ('fsdp', 'replica')), may hold values from -6 to 6
- kv_weight: bfloat16 [8192, 2, 1024], P(('fsdp', 'replica'), None, 'tensor'), may hold values from -0.0625 to 0.0625
- queries: bfloat16 [4, 128, 8192], P(None, ('fsdp', 'replica'), 'tensor'), may hold values from -360 to 360, as said below
- key_cache: bfloat16 [128, 2048, 1024], P(('fsdp', 'replica'), 'tensor'), may hold values from -6 to 6
- value_cache: bfloat16 [128, 2048, 1024], P(('fsdp', 'replica'), 'tensor'), may hold values from -6 to 6
- lengths: int32 [128], P(('fsdp', 'replica')), may hold values from 1 to 2044, as said below
Outputs:
- attended: bfloat16 [4, 128, 8192], P(None, ('fsdp', 'replica'), 'tensor')
- new_keys: bfloat16 [4, 128, 1024], P(None, ('fsdp', 'replica'), 'tensor')
- new_values: bfloat16 [4, 128, 1024], P(None, ('fsdp', 'replica'), 'tensor')
The draws below stay inside these ranges and needn't reach their ends.
Inputs may be any that keep to these rules, and one draw needn't show every extreme that they name: Entries of queries stay within the bounds. Row r's cache is valid at positions below lengths[r]; some row has exactly 2044, some row has 1.
All inputs are finite; a program needn't handle non-finite values.
Results may differ from the reference program's by a relative error of at most 0.013.
Values may be sent and summed in bfloat16 or wider, within the bound.
No kernel may reach another device: no remote copies, remote signals or barrier semaphores. Data moves between devices by JAX's collectives and lax.ppermute only.
A program may use at most 64 MiB of HBM per device.

```python
import jax
import jax.numpy as jnp
from jax import lax

D = 8192
KVH = 8
HQ = 64
HD = 128
STEPS = 4
CACHE = 2048
ROWS = 128


def draw_queries(key, part):
    key = jax.random.fold_in(key, 11)
    base = jnp.clip(jax.random.normal(key, (STEPS, ROWS, HQ, HD), jnp.float32), -6.0, 6.0)
    return base.reshape(STEPS, ROWS, HQ * HD).astype(jnp.bfloat16)


def draw_lengths(key, part):
    key = jax.random.fold_in(key, 23)
    drawn = jax.random.randint(key, (ROWS,), 1, CACHE - STEPS + 1, jnp.int32)
    return drawn.at[0].set(CACHE - STEPS).at[1].set(1)


def shard_levels(stream_key, dims, cuts, smallest, largest):
    loudness, own = 1.0, jax.random.fold_in(stream_key, 6)
    for dim, shards_of in cuts:
        draws = jnp.exp(jax.random.uniform(jax.random.fold_in(own, dim), (shards_of,), jnp.float32, smallest / len(cuts), largest / len(cuts)))
        loudness = loudness * jnp.repeat(draws, dims[dim] // shards_of).reshape([-1 if axis == dim else 1 for axis in range(len(dims))])
    return loudness


def bell_draw(key, extent, spread, limit, cuts=(), kind=jnp.bfloat16):
    values = jax.random.normal(key, extent, jnp.float32) * spread
    if len(cuts) > 0:
        values = shard_levels(key, extent, cuts, -0.22, 0.18) * values
    return jnp.clip(values, min=-limit, max=limit).astype(kind)


def setup_inputs(seed: int = 0) -> dict:
    key_of = jax.random.split(jax.random.key(seed), 7)
    return {
        "hidden": bell_draw(key_of[0], (STEPS, ROWS, D), 1.0, 6.0, ((1, 128),)),
        "kv_weight": bell_draw(key_of[1], (D, 2, KVH * HD), D ** -0.5, 0.0625, ((0, 128), (2, 4))),
        "queries": draw_queries(jax.random.fold_in(key_of[6], 71), 0),
        "key_cache": bell_draw(key_of[3], (ROWS, CACHE, KVH * HD), 1.0, 6.0, ((0, 128), (1, 4))),
        "value_cache": bell_draw(key_of[4], (ROWS, CACHE, KVH * HD), 1.0, 6.0, ((0, 128), (1, 4))),
        "lengths": draw_lengths(jax.random.fold_in(key_of[6], 71), 0),
    }


ROPE_BASE = 500000.0
NEG_FILL = -1e30


def rotate(vectors, positions, head_count):
    step_count, row_count, width_all = vectors.shape
    head_size = width_all // head_count
    half_size = head_size // 2
    frequency = ROPE_BASE ** (-jnp.arange(half_size, dtype=jnp.float32) * 2.0 / head_size)
    phases = positions.astype(jnp.float32)[:, :, None] * frequency[None, None, :]
    cos_part = jnp.cos(phases)[:, :, None, :]
    sin_part = jnp.sin(phases)[:, :, None, :]
    heads_view = vectors.reshape(step_count, row_count, head_count, head_size)
    front_half = heads_view[..., :half_size]
    back_half = heads_view[..., half_size:]
    turned = jnp.concatenate([front_half * cos_part - back_half * sin_part, front_half * sin_part + back_half * cos_part], axis=-1)
    return turned.reshape(step_count, row_count, width_all)


def attend_row(row_items):
    query_row, key_row, value_row, fresh_keys, fresh_values, length = row_items
    group_size = HQ // KVH
    query_view = query_row.astype(jnp.float32).reshape(STEPS, KVH, group_size, HD)
    every_key = jnp.concatenate([key_row, fresh_keys], axis=0).astype(jnp.float32).reshape(CACHE + STEPS, KVH, HD)
    every_value = jnp.concatenate([value_row, fresh_values], axis=0).astype(jnp.float32).reshape(CACHE + STEPS, KVH, HD)
    scores = jnp.einsum('shgd,chd->shgc', query_view, every_key, precision=lax.Precision.HIGHEST) * (HD ** -0.5)
    position = jnp.arange(CACHE + STEPS, dtype=jnp.int32)
    cache_allowed = jnp.broadcast_to(position[None, :] < length, (STEPS, CACHE + STEPS))
    fresh_allowed = (position[None, :] - CACHE) <= jnp.arange(STEPS, dtype=jnp.int32)[:, None]
    allowed = jnp.where(position[None, :] < CACHE, cache_allowed, fresh_allowed)[:, None, None, :]
    masked = jnp.where(allowed, scores, NEG_FILL)
    maxima = jnp.max(masked, axis=-1, keepdims=True)
    weights = jnp.where(allowed, jnp.exp(masked - maxima), 0.0)
    totals = jnp.sum(weights, axis=-1)
    rounded = weights.astype(jnp.bfloat16).astype(jnp.float32)
    summed = jnp.einsum('shgc,chd->shgd', rounded, every_value, precision=lax.Precision.HIGHEST)
    return (summed / totals[..., None]).reshape(STEPS, HQ * HD).astype(jnp.bfloat16)


def reference(hidden, kv_weight, queries, key_cache, value_cache, lengths):
    flat_rows = hidden.reshape(STEPS * ROWS, D)
    projected = jnp.dot(flat_rows, kv_weight.reshape(D, 2 * KVH * HD), preferred_element_type=jnp.float32)
    projected = projected.reshape(STEPS, ROWS, 2, KVH * HD)
    positions = lengths[None, :] + jnp.arange(STEPS, dtype=jnp.int32)[:, None]
    new_keys = rotate(projected[:, :, 0], positions, KVH).astype(jnp.bfloat16)
    new_values = projected[:, :, 1].astype(jnp.bfloat16)
    per_row = lax.map(attend_row, (jnp.transpose(queries, (1, 0, 2)), key_cache, value_cache, jnp.transpose(new_keys, (1, 0, 2)), jnp.transpose(new_values, (1, 0, 2)), lengths))
    attended = jnp.transpose(per_row, (1, 0, 2))
    return attended, new_keys, new_values
```

```python
import jax
import jax.numpy as jnp
from jax import lax
from jax.experimental import pallas as pl
from jax.experimental.pallas import tpu as pltpu
from jax.sharding import Mesh
from jax.sharding import PartitionSpec as P

KVH = 8
HQ = 64
HD = 128
STEPS = 4
GROUP = HQ // KVH
TENSOR = 4
LOCAL_HEADS = KVH // TENSOR
HEAD_ROWS = STEPS * GROUP
OWN_ROWS = LOCAL_HEADS * HEAD_ROWS
ROPE_BASE = 500000.0
NEG_FILL = -1e30
F32 = jnp.float32
BF16 = jnp.bfloat16
PARAMS = pltpu.CompilerParams(vmem_limit_bytes=16 * 1024 * 1024)
ROWS_AXES = ("zlo", "core", "x", "zhi")
Z_AXES = ("zhi", "zlo")


def lane_iota(shape):
    return lax.broadcasted_iota(jnp.int32, shape, 1)


def prepare_kernel(hidden_ref, queries_ref, hidden_out, queries_out, rows):
    low = lane_iota((STEPS, 128)) < 64
    for zlo in range(8):
        for pair in range(4):
            at = zlo * 1024 + pair * 256
            one = hidden_ref[:, 0, at : at + 128].astype(F32)
            two = hidden_ref[:, 0, at + 128 : at + 256].astype(F32)
            to = slice(pair * 128, pair * 128 + 128)
            hidden_out[zlo, :, to] = jnp.where(low, one, pltpu.roll(two, 64, 1)).astype(BF16)
            hidden_out[8 + zlo, :, to] = jnp.where(low, pltpu.roll(one, 64, 1), two).astype(BF16)
    for head in range(LOCAL_HEADS):
        for member in range(GROUP):
            at = (head * GROUP + member) * HD
            block = queries_ref[:, 0, at : at + HD].astype(F32)
            for step in range(STEPS):
                row = head * HEAD_ROWS + step * GROUP + member
                rows[row : row + 1, :] = block[step : step + 1, :]
    packed = rows[...].astype(BF16)
    for to in range(TENSOR):
        queries_out[to] = packed


def prepare(hidden, queries):
    return pl.pallas_call(
        prepare_kernel,
        out_shape=(
            jax.ShapeDtypeStruct((16, STEPS, 512), BF16),
            jax.ShapeDtypeStruct((TENSOR, OWN_ROWS, HD), BF16),
        ),
        scratch_shapes=[pltpu.VMEM((OWN_ROWS, HD), F32)],
        compiler_params=PARAMS,
        name="prepare",
    )(hidden, queries)


def attend_kernel(place_ref, queries_ref, keys_ref, values_ref, out_ref, spread):
    spread[...] = jnp.zeros_like(spread)
    for head in range(KVH):
        piece = queries_ref[head // 2, (head % 2) * HEAD_ROWS : (head % 2 + 1) * HEAD_ROWS, :]
        spread[head * HEAD_ROWS : (head + 1) * HEAD_ROWS, head * HD : (head + 1) * HD] = piece
    scores = lax.dot_general(
        keys_ref[0], spread[...], (((1,), (1,)), ((), ())), preferred_element_type=F32
    ) * (HD**-0.5)
    position = place_ref[0] + lax.broadcasted_iota(jnp.int32, scores.shape, 0)
    allowed = position < place_ref[1]
    masked = jnp.where(allowed, scores, NEG_FILL)
    maxima = jnp.max(masked, axis=0, keepdims=True)
    weights = jnp.where(allowed, jnp.exp(masked - maxima), 0.0)
    totals = jnp.sum(weights, axis=0, keepdims=True)
    rounded = weights.astype(BF16)
    for half in range(2):
        summed = lax.dot_general(
            rounded[:, half * 128 : half * 128 + 128],
            values_ref[0, :, half * 512 : half * 512 + 512],
            (((0,), (0,)), ((), ())),
            preferred_element_type=F32,
        )
        for inner in range(4):
            head = half * 4 + inner
            out_ref[head // 2, (head % 2) * HEAD_ROWS : (head % 2 + 1) * HEAD_ROWS, :] = summed[
                inner * HEAD_ROWS : (inner + 1) * HEAD_ROWS, inner * HD : (inner + 1) * HD
            ]
    for to in range(TENSOR):
        span = slice((to // 2) * 128, (to // 2) * 128 + 128)
        pair = jnp.concatenate([maxima[:, span], totals[:, span]], axis=0)
        if to % 2:
            pair = pltpu.roll(pair, 64, 1)
        out_ref[to, OWN_ROWS : OWN_ROWS + 2, :] = pair


def attend(place, queries, keys, values):
    whole = pl.BlockSpec(memory_space=pltpu.VMEM)
    return pl.pallas_call(
        attend_kernel,
        out_shape=jax.ShapeDtypeStruct((TENSOR, OWN_ROWS + 8, HD), F32),
        in_specs=[pl.BlockSpec(memory_space=pltpu.SMEM), whole, whole, whole],
        out_specs=whole,
        scratch_shapes=[pltpu.VMEM((KVH * HEAD_ROWS, KVH * HD), BF16)],
        compiler_params=PARAMS,
        cost_estimate=pl.CostEstimate(
            flops=2 * 2 * 512 * 1024 * 256, bytes_accessed=5 << 20, transcendentals=512 * 256
        ),
        name="attend",
    )(place, queries, keys, values)


def project_kernel(place_ref, hidden_ref, own_ref, other_ref, out_ref, tokens):
    for z in range(16):
        tokens[z * STEPS : (z + 1) * STEPS, :] = hidden_ref[z].astype(F32)
    first = tokens[:, :256]
    second = tokens[:, 256:]
    swap = place_ref[2] == 1
    own = jnp.where(swap, second, first).astype(BF16)
    other = jnp.where(swap, first, second).astype(BF16)
    partial = jnp.dot(own, own_ref[...].reshape(256, 512), preferred_element_type=F32)
    partial += jnp.dot(other, other_ref[...].reshape(256, 512), preferred_element_type=F32)
    for z in range(16):
        out_ref[z] = partial[z * STEPS : (z + 1) * STEPS, :]


def project(place, hidden, own, other):
    whole = pl.BlockSpec(memory_space=pltpu.VMEM)
    return pl.pallas_call(
        project_kernel,
        out_shape=jax.ShapeDtypeStruct((16, STEPS, 512), F32),
        in_specs=[pl.BlockSpec(memory_space=pltpu.SMEM), whole, whole, whole],
        out_specs=whole,
        scratch_shapes=[pltpu.VMEM((64, 512), F32)],
        compiler_params=PARAMS,
        cost_estimate=pl.CostEstimate(
            flops=2 * 64 * 512 * 512, bytes_accessed=1 << 20, transcendentals=0
        ),
        name="project",
    )(place, hidden, own, other)


def finish_kernel(
    parts_ref, sums_ref, queries_ref, cos_ref, sin_ref, attended_ref, keys_ref, values_ref, wide
):
    projected = jnp.sum(sums_ref[...], axis=0)
    cos_part = cos_ref[...]
    sin_part = sin_ref[...]
    new_values = projected[:, 256:].astype(BF16)
    values_ref[:, 0, :] = new_values
    queries = queries_ref[0]
    fresh = []
    for head in range(LOCAL_HEADS):
        front = projected[:, head * HD : (head + 1) * HD]
        turned = (front * cos_part + pltpu.roll(front, HD // 2, 1) * sin_part).astype(BF16)
        keys_ref[:, 0, head * HD : (head + 1) * HD] = turned
        fresh.append(
            lax.dot_general(
                turned, queries, (((1,), (1,)), ((), ())), preferred_element_type=F32
            )
        )
    lane = lane_iota((STEPS, OWN_ROWS))
    scores = jnp.where(lane < HEAD_ROWS, fresh[0], fresh[1]) * (HD**-0.5)
    step = (lane % HEAD_ROWS) // GROUP
    allowed = lax.broadcasted_iota(jnp.int32, (STEPS, OWN_ROWS), 0) <= step
    masked = jnp.where(allowed, scores, NEG_FILL)
    maxima = [parts_ref[t, OWN_ROWS : OWN_ROWS + 1, :OWN_ROWS] for t in range(TENSOR)]
    joined = jnp.max(masked, axis=0, keepdims=True)
    for part in maxima:
        joined = jnp.maximum(joined, part)
    weights = jnp.where(allowed, jnp.exp(masked - joined), 0.0)
    totals = jnp.sum(weights, axis=0, keepdims=True)
    scales = []
    for t in range(TENSOR):
        scale = jnp.exp(maxima[t] - joined)
        totals += parts_ref[t, OWN_ROWS + 1 : OWN_ROWS + 2, :OWN_ROWS] * scale
        scales.append(scale)
    factors = jnp.concatenate([*scales, weights.astype(BF16).astype(F32)], axis=0) / totals
    factors = jnp.concatenate([factors, jnp.zeros((8, 128 - OWN_ROWS), F32)], axis=1)
    columns = jnp.transpose(factors, (1, 0))
    values = new_values.astype(F32)
    for head in range(LOCAL_HEADS):
        rows = slice(head * HEAD_ROWS, (head + 1) * HEAD_ROWS)
        total = jnp.zeros((HEAD_ROWS, HD), F32)
        for t in range(TENSOR):
            total += parts_ref[t, rows, :] * columns[rows, t : t + 1]
        for t in range(STEPS):
            total += columns[rows, 4 + t : 5 + t] * values[t : t + 1, head * HD : (head + 1) * HD]
        for s in range(STEPS):
            for member in range(GROUP):
                at = (head * GROUP + member) * HD
                row = s * GROUP + member
                wide[s : s + 1, at : at + HD] = total[row : row + 1, :]
    attended_ref[:, 0, :] = wide[...].astype(BF16)


def finish(parts, sums, queries, cos_part, sin_part):
    return pl.pallas_call(
        finish_kernel,
        out_shape=(
            jax.ShapeDtypeStruct((STEPS, 1, LOCAL_HEADS * GROUP * HD), BF16),
            jax.ShapeDtypeStruct((STEPS, 1, LOCAL_HEADS * HD), BF16),
            jax.ShapeDtypeStruct((STEPS, 1, LOCAL_HEADS * HD), BF16),
        ),
        scratch_shapes=[pltpu.VMEM((STEPS, LOCAL_HEADS * GROUP * HD), F32)],
        compiler_params=PARAMS,
        name="finish",
    )(parts, sums, queries, cos_part, sin_part)


def rotation(lengths):
    half = HD // 2
    positions = lengths[None, :] + jnp.arange(STEPS, dtype=jnp.int32)[:, None]
    frequency = ROPE_BASE ** (-jnp.arange(half, dtype=F32) * 2.0 / HD)
    phases = positions.astype(F32) * frequency[None, :]
    cos_part = jnp.cos(phases)
    sin_part = jnp.sin(phases)
    return (
        jnp.concatenate([cos_part, cos_part], axis=-1),
        jnp.concatenate([-sin_part, sin_part], axis=-1),
    )


def body(hidden, kv_weight, queries, key_cache, value_cache, lengths):
    place = jnp.stack([lax.axis_index("tensor") * 512, lengths[0], lax.axis_index("core")])
    spread_hidden, spread_queries = prepare(hidden, queries)
    weight = kv_weight.reshape(1, 64, 512)
    own = lax.all_to_all(jnp.broadcast_to(weight, (4, 64, 512)), "x", 0, 0)
    tokens = lax.all_to_all(spread_hidden, Z_AXES, 0, 0)
    all_queries = lax.all_to_all(spread_queries, "tensor", 0, 0)
    other = lax.ppermute(own, "core", [(0, 1), (1, 0)])
    partial = project(place, tokens, own, other)
    sums = lax.all_to_all(partial, Z_AXES, 0, 0)
    parts = attend(place, all_queries, key_cache, value_cache)
    parts = lax.all_to_all(parts, "tensor", 0, 0)
    cos_part, sin_part = rotation(lengths)
    return finish(parts, sums, spread_queries, cos_part, sin_part)


def solution(mesh):
    split = Mesh(mesh.devices.reshape(8, 2, 4, 4, 2), ("zlo", "core", "tensor", "x", "zhi"))
    return jax.shard_map(
        body,
        mesh=split,
        in_specs=(
            P(None, ROWS_AXES, None),
            P(ROWS_AXES, None, "tensor"),
            P(None, ROWS_AXES, "tensor"),
            P(ROWS_AXES, "tensor", None),
            P(ROWS_AXES, "tensor", None),
            P(ROWS_AXES),
        ),
        out_specs=(
            P(None, ROWS_AXES, "tensor"),
            P(None, ROWS_AXES, "tensor"),
            P(None, ROWS_AXES, "tensor"),
        ),
        check_vma=False,
    )
```

```python
import jax
import jax.numpy as jnp
from jax import lax
from jax.experimental import pallas as pl
from jax.experimental.pallas import tpu as pltpu
from jax.sharding import Mesh
from jax.sharding import PartitionSpec as P

KVH = 8
HQ = 64
HD = 128
STEPS = 4
GROUP = HQ // KVH
TENSOR = 4
LOCAL_HEADS = KVH // TENSOR
HEAD_ROWS = STEPS * GROUP
OWN_ROWS = LOCAL_HEADS * HEAD_ROWS
ROPE_BASE = 500000.0
NEG_FILL = -1e30
F32 = jnp.float32
BF16 = jnp.bfloat16
PARAMS = pltpu.CompilerParams(vmem_limit_bytes=16 * 1024 * 1024)
WIDE = pltpu.CompilerParams(vmem_limit_bytes=66_100_000)
ROWS_AXES = ("zlo", "core", "x", "zhi")
Z_AXES = ("zhi", "zlo")
Z_FIRST = 12
Z_GROUPS = [[(Z_FIRST + i) % 16 for i in range(16)]]


def lane_iota(shape):
    return lax.broadcasted_iota(jnp.int32, shape, 1)


SMEM = pl.BlockSpec(memory_space=pltpu.SMEM)
VMEM = pl.BlockSpec(memory_space=pltpu.VMEM)
HBM = pl.BlockSpec(memory_space=pltpu.HBM)


def gate(values, *after):
    return lax.optimization_barrier((values, *after))[0]


def prepare_kernel(
    hidden_hbm, queries_hbm, hidden_out, queries_out, rows, hidden_ref, queries_ref, sems
):
    query_copy = pltpu.make_async_copy(queries_hbm, queries_ref, sems.at[0])
    hidden_copy = pltpu.make_async_copy(hidden_hbm, hidden_ref, sems.at[1])
    query_copy.start()
    hidden_copy.start()
    query_copy.wait()
    for head in range(LOCAL_HEADS):
        for member in range(GROUP):
            at = (head * GROUP + member) * HD
            piece = queries_ref[:, at : at + HD].astype(F32)
            for step in range(STEPS):
                row = head * HEAD_ROWS + step * GROUP + member
                rows[row : row + 1, :] = piece[step : step + 1, :]
    queries_out[...] = rows[...].astype(BF16)
    hidden_copy.wait()
    low = lane_iota((STEPS, 128)) < 64
    for zlo in range(8):
        for pair in range(4):
            at = zlo * 1024 + pair * 256
            one = hidden_ref[:, at : at + 128].astype(F32)
            two = hidden_ref[:, at + 128 : at + 256].astype(F32)
            to = slice(pair * 128, pair * 128 + 128)
            even = jnp.where(low, one, pltpu.roll(two, 64, 1)).astype(BF16)
            odd = jnp.where(low, pltpu.roll(one, 64, 1), two).astype(BF16)
            hidden_out[(zlo - Z_FIRST) % 16, :, to] = even
            hidden_out[(8 + zlo - Z_FIRST) % 16, :, to] = odd


def prepare(hidden, queries):
    return pl.pallas_call(
        prepare_kernel,
        out_shape=(
            jax.ShapeDtypeStruct((16, STEPS, 512), BF16),
            jax.ShapeDtypeStruct((OWN_ROWS, HD), BF16),
        ),
        in_specs=[HBM, HBM],
        out_specs=(VMEM, VMEM),
        scratch_shapes=[
            pltpu.VMEM((OWN_ROWS, HD), F32),
            pltpu.VMEM(hidden.shape, BF16),
            pltpu.VMEM(queries.shape, BF16),
            pltpu.SemaphoreType.DMA((2,)),
        ],
        compiler_params=WIDE,
        cost_estimate=pl.CostEstimate(flops=1 << 16, bytes_accessed=1 << 18, transcendentals=0),
        name="prepare",
    )(hidden, queries)


ORDER = (0, 1, 3, 2)


def attend_kernel(
    place_ref, near_ref, far_ref, keys_ref, values_ref, kept_ref, sent_ref, spread
):
    tensor = place_ref[0]
    spread[...] = jnp.zeros_like(spread)
    starts = []
    for k in range(TENSOR):
        start = (tensor ^ ORDER[k]) * (LOCAL_HEADS * HD)
        starts.append(start)
        for head in range(LOCAL_HEADS):
            lanes = pl.ds(pl.multiple_of(start + head * HD, HD), HD)
            at = (k % 2) * OWN_ROWS + head * HEAD_ROWS
            to = k * OWN_ROWS + head * HEAD_ROWS
            piece = (near_ref, far_ref)[k // 2][at : at + HEAD_ROWS, :]
            spread[to : to + HEAD_ROWS, lanes] = piece
    scores = lax.dot_general(
        keys_ref[0], spread[...], (((1,), (1,)), ((), ())), preferred_element_type=F32
    ) * (HD**-0.5)
    held = scores.shape[0]
    position = tensor * held + lax.broadcasted_iota(jnp.int32, scores.shape, 0)
    allowed = position < place_ref[1]
    masked = jnp.where(allowed, scores, NEG_FILL)
    maxima = jnp.max(masked, axis=0, keepdims=True)
    weights = jnp.where(allowed, jnp.exp(masked - maxima), 0.0)
    totals = jnp.sum(weights, axis=0, keepdims=True)
    rounded = weights.astype(BF16)
    for half, out_ref in enumerate((kept_ref, sent_ref)):
        span = slice(half * 128, half * 128 + 128)
        values = jnp.concatenate(
            [
                values_ref[0, :, pl.ds(pl.multiple_of(starts[2 * half + n], 256), 256)]
                for n in range(2)
            ],
            axis=1,
        )
        summed = lax.dot_general(
            rounded[:, span], values, (((0,), (0,)), ((), ())), preferred_element_type=F32
        )
        pair = jnp.concatenate([maxima[:, span], totals[:, span]], axis=0)
        for n in range(2):
            for head in range(LOCAL_HEADS):
                at = n * LOCAL_HEADS + head
                out_ref[n, head * HEAD_ROWS : (head + 1) * HEAD_ROWS, :] = summed[
                    at * HEAD_ROWS : (at + 1) * HEAD_ROWS, at * HD : (at + 1) * HD
                ]
            out_ref[n, OWN_ROWS : OWN_ROWS + 2, :] = pltpu.roll(pair, 64, 1) if n else pair


def attend(place, near, far, keys, values):
    return pl.pallas_call(
        attend_kernel,
        out_shape=(jax.ShapeDtypeStruct((2, OWN_ROWS + 8, HD), F32),) * 2,
        in_specs=[SMEM, VMEM, VMEM, VMEM, VMEM],
        out_specs=(VMEM, VMEM),
        scratch_shapes=[pltpu.VMEM((KVH * HEAD_ROWS, KVH * HD), BF16)],
        compiler_params=PARAMS,
        cost_estimate=pl.CostEstimate(flops=1, bytes_accessed=1, transcendentals=0),
        name="attend",
    )(place, near, far, keys, values)


def merge_kernel(kept_ref, come_ref, own_ref, next_ref):
    rows = []
    for n in range(2):
        stats = [ref[n, OWN_ROWS : OWN_ROWS + 2, :] for ref in (kept_ref, come_ref)]
        joined = jnp.maximum(stats[0][:1], stats[1][:1])
        scales = [jnp.exp(stat[:1] - joined) for stat in stats]
        total = stats[0][1:] * scales[0] + stats[1][1:] * scales[1]
        out_ref = (own_ref, next_ref)[n]
        out_ref[OWN_ROWS : OWN_ROWS + 2, :] = jnp.concatenate([joined, total], axis=0)
        rows += scales
    columns = jnp.transpose(jnp.concatenate(rows + rows, axis=0), (1, 0))
    for n in range(2):
        out_ref = (own_ref, next_ref)[n]
        out_ref[:OWN_ROWS, :] = (
            kept_ref[n, :OWN_ROWS, :] * columns[:OWN_ROWS, 2 * n : 2 * n + 1]
            + come_ref[n, :OWN_ROWS, :] * columns[:OWN_ROWS, 2 * n + 1 : 2 * n + 2]
        )


def merge(kept, come):
    return pl.pallas_call(
        merge_kernel,
        out_shape=(jax.ShapeDtypeStruct((OWN_ROWS + 8, HD), F32),) * 2,
        in_specs=[VMEM, VMEM],
        out_specs=(VMEM, VMEM),
        compiler_params=PARAMS,
        cost_estimate=pl.CostEstimate(
            flops=1 << 17, bytes_accessed=1 << 18, transcendentals=1 << 9
        ),
        name="merge",
    )(kept, come)


def project_kernel(place_ref, hidden_ref, own_ref, other_ref, out_ref, tokens):
    core = place_ref[2]
    x = place_ref[3]
    odd = x % 2 == 1
    for z in range(16):
        tokens[z * STEPS : (z + 1) * STEPS, :] = hidden_ref[z].astype(F32)
    partial = jnp.zeros((16 * STEPS, 512), F32)
    for swap, weight_ref in enumerate((own_ref, other_ref)):
        for pair in range(2):
            at = (core ^ swap) * 256 + ((x // 2) ^ pair) * 128
            block = tokens[:, pl.ds(pl.multiple_of(at, 128), 128)]
            turned = pltpu.roll(block, 64, 1)
            block = jnp.where(odd, *((block, turned) if pair else (turned, block)))
            partial += jnp.dot(
                block.astype(BF16),
                weight_ref[pair * 128 : pair * 128 + 128, :],
                preferred_element_type=F32,
            )
    for z in range(16):
        out_ref[z] = partial[z * STEPS : (z + 1) * STEPS, :]


def project(place, hidden, own, other):
    return pl.pallas_call(
        project_kernel,
        out_shape=jax.ShapeDtypeStruct((16, STEPS, 512), F32),
        in_specs=[SMEM, VMEM, VMEM, VMEM],
        out_specs=VMEM,
        scratch_shapes=[pltpu.VMEM((64, 512), F32)],
        compiler_params=PARAMS,
        cost_estimate=pl.CostEstimate(
            flops=2 * 64 * 512 * 512, bytes_accessed=1 << 20, transcendentals=0
        ),
        name="project",
    )(place, hidden, own, other)


def finish_kernel(
    part0_ref,
    part1_ref,
    sums_ref,
    queries_ref,
    cos_ref,
    sin_ref,
    attended_ref,
    keys_ref,
    values_ref,
    wide,
):
    parts = (part0_ref, part1_ref)
    projected = jnp.sum(sums_ref[...], axis=0)
    cos_part = cos_ref[...]
    sin_part = sin_ref[...]
    new_values = projected[:, LOCAL_HEADS * HD :].astype(BF16)
    values_ref[...] = new_values
    queries = queries_ref[:OWN_ROWS]
    fresh = []
    for head in range(LOCAL_HEADS):
        front = projected[:, head * HD : (head + 1) * HD]
        turned = (front * cos_part + pltpu.roll(front, HD // 2, 1) * sin_part).astype(BF16)
        keys_ref[:, head * HD : (head + 1) * HD] = turned
        fresh.append(
            lax.dot_general(
                turned, queries, (((1,), (1,)), ((), ())), preferred_element_type=F32
            )
        )
    lane = lane_iota((STEPS, OWN_ROWS))
    scores = jnp.where(lane < HEAD_ROWS, fresh[0], fresh[1]) * (HD**-0.5)
    step = (lane % HEAD_ROWS) // GROUP
    allowed = lax.broadcasted_iota(jnp.int32, (STEPS, OWN_ROWS), 0) <= step
    masked = jnp.where(allowed, scores, NEG_FILL)
    maxima = [part[OWN_ROWS : OWN_ROWS + 1, :OWN_ROWS] for part in parts]
    joined = jnp.max(masked, axis=0, keepdims=True)
    for part in maxima:
        joined = jnp.maximum(joined, part)
    weights = jnp.where(allowed, jnp.exp(masked - joined), 0.0)
    totals = jnp.sum(weights, axis=0, keepdims=True)
    scales = []
    for t in range(len(parts)):
        scale = jnp.exp(maxima[t] - joined)
        totals += parts[t][OWN_ROWS + 1 : OWN_ROWS + 2, :OWN_ROWS] * scale
        scales.append(scale)
    factors = jnp.concatenate([*scales, weights.astype(BF16).astype(F32)], axis=0) / totals
    factors = jnp.concatenate([factors, jnp.zeros((6, 128 - OWN_ROWS), F32)], axis=1)
    factors = jnp.concatenate([factors, jnp.zeros((2, 128), F32)], axis=0)
    columns = jnp.transpose(factors, (1, 0))
    values = new_values.astype(F32)
    for head in range(LOCAL_HEADS):
        rows = slice(head * HEAD_ROWS, (head + 1) * HEAD_ROWS)
        total = jnp.zeros((HEAD_ROWS, HD), F32)
        for t in range(len(parts)):
            total += parts[t][rows, :] * columns[rows, t : t + 1]
        for t in range(STEPS):
            total += columns[rows, 2 + t : 3 + t] * values[t : t + 1, head * HD : (head + 1) * HD]
        for s in range(STEPS):
            for member in range(GROUP):
                at = (head * GROUP + member) * HD
                row = s * GROUP + member
                wide[s : s + 1, at : at + HD] = total[row : row + 1, :]
    attended_ref[...] = wide[...].astype(BF16)


def finish(parts, sums, queries, cos_part, sin_part):
    return pl.pallas_call(
        finish_kernel,
        out_shape=(
            jax.ShapeDtypeStruct((STEPS, LOCAL_HEADS * GROUP * HD), BF16),
            jax.ShapeDtypeStruct((STEPS, LOCAL_HEADS * HD), BF16),
            jax.ShapeDtypeStruct((STEPS, LOCAL_HEADS * HD), BF16),
        ),
        in_specs=[VMEM] * 6,
        out_specs=(VMEM,) * 3,
        scratch_shapes=[pltpu.VMEM((STEPS, LOCAL_HEADS * GROUP * HD), F32)],
        compiler_params=PARAMS,
        cost_estimate=pl.CostEstimate(
            flops=1 << 20, bytes_accessed=1 << 19, transcendentals=1 << 10
        ),
        name="finish",
    )(*parts, sums, queries, cos_part, sin_part)


def rotation(lengths):
    half = HD // 2
    positions = lengths[None, :] + jnp.arange(STEPS, dtype=jnp.int32)[:, None]
    frequency = ROPE_BASE ** (-jnp.arange(half, dtype=F32) * 2.0 / HD)
    phases = positions.astype(F32) * frequency[None, :]
    cos_part = jnp.cos(phases)
    sin_part = jnp.sin(phases)
    return (
        jnp.concatenate([cos_part, cos_part], axis=-1),
        jnp.concatenate([-sin_part, sin_part], axis=-1),
    )


def exchange_z(blocks):
    return lax.all_to_all(blocks, Z_AXES, 0, 0, axis_index_groups=Z_GROUPS)


def with_partner(values, axis, flip, size=4):
    return lax.ppermute(values, axis, [(i, i ^ flip) for i in range(size)])


def body(hidden, kv_weight, queries, key_cache, value_cache, lengths):
    place = jnp.stack(
        [lax.axis_index("tensor"), lengths[0], lax.axis_index("core"), lax.axis_index("x")]
    )
    chunks, own_queries = prepare(hidden.reshape(STEPS, -1), queries.reshape(STEPS, -1))
    weight = kv_weight.reshape(64, 512)
    come = with_partner(weight, "x", 1)
    weight = jnp.concatenate([weight, come], axis=0)
    near = jnp.concatenate([own_queries, with_partner(own_queries, "tensor", 1)], axis=0)
    tokens = exchange_z(gate(chunks, come))
    far = with_partner(near, "tensor", 3)
    weight = jnp.concatenate([weight, with_partner(weight, "x", 3)], axis=0)
    kept, sent = attend(place, near, far, key_cache, value_cache)
    other = with_partner(gate(weight, tokens, kept), "core", 1, 2)
    partial = project(place, tokens, weight, other)
    sums = exchange_z(partial)
    own_part, next_part = merge(kept, with_partner(sent, "tensor", 3))
    parts = (own_part, with_partner(next_part, "tensor", 1))
    cos_part, sin_part = rotation(lengths)
    outs = finish(parts, sums, near, cos_part, sin_part)
    return tuple(out.reshape(STEPS, 1, -1) for out in outs)


def solution(mesh):
    split = Mesh(mesh.devices.reshape(8, 2, 4, 4, 2), ("zlo", "core", "tensor", "x", "zhi"))
    return jax.shard_map(
        body,
        mesh=split,
        in_specs=(
            P(None, ROWS_AXES, None),
            P(ROWS_AXES, None, "tensor"),
            P(None, ROWS_AXES, "tensor"),
            P(ROWS_AXES, "tensor", None),
            P(ROWS_AXES, "tensor", None),
            P(ROWS_AXES),
        ),
        out_specs=(
            P(None, ROWS_AXES, "tensor"),
            P(None, ROWS_AXES, "tensor"),
            P(None, ROWS_AXES, "tensor"),
        ),
        check_vma=False,
    )
```

```python
import jax
import jax.numpy as jnp
from jax import lax
from jax.experimental import pallas as pl
from jax.experimental.pallas import tpu as pltpu
from jax.sharding import Mesh
from jax.sharding import PartitionSpec as P

KVH = 8
HQ = 64
HD = 128
STEPS = 4
GROUP = HQ // KVH
TENSOR = 4
LOCAL_HEADS = KVH // TENSOR
HEAD_ROWS = STEPS * GROUP
OWN_ROWS = LOCAL_HEADS * HEAD_ROWS
ROPE_BASE = 500000.0
NEG_FILL = -1e30
F32 = jnp.float32
BF16 = jnp.bfloat16
PARAMS = pltpu.CompilerParams(vmem_limit_bytes=16 * 1024 * 1024)
ROWS_AXES = ("zlo", "core", "x", "zhi")
Z_AXES = ("zhi", "zlo")
def ring(first):
    return [(first + hops) % 16 for hops in range(16)]


TOKENS_ORDER = ring(11)
SUMS_ORDER = ring(0)


def lane_iota(shape):
    return lax.broadcasted_iota(jnp.int32, shape, 1)


SMEM = pl.BlockSpec(memory_space=pltpu.SMEM)
VMEM = pl.BlockSpec(memory_space=pltpu.VMEM)
HBM = pl.BlockSpec(memory_space=pltpu.HBM)


def gate(values, *after):
    return lax.optimization_barrier((values, *after))[0]


def in_hbm(array):
    return pltpu.with_memory_space_constraint(array, pltpu.HBM)


def prepare_kernel(
    hidden_hbm, queries_hbm, hidden_out, queries_out, rows, hidden_ref, queries_ref, sems
):
    query_copy = pltpu.make_async_copy(queries_hbm, queries_ref, sems.at[0])
    hidden_copy = pltpu.make_async_copy(hidden_hbm, hidden_ref, sems.at[1])
    query_copy.start()
    hidden_copy.start()
    query_copy.wait()
    for head in range(LOCAL_HEADS):
        for member in range(GROUP):
            at = (head * GROUP + member) * HD
            piece = queries_ref[:, at : at + HD].astype(F32)
            for step in range(STEPS):
                row = head * HEAD_ROWS + step * GROUP + member
                rows[row : row + 1, :] = piece[step : step + 1, :]
    queries_out[...] = rows[...].astype(BF16)
    hidden_copy.wait()
    low = lane_iota((STEPS, 128)) < 64
    for zlo in range(8):
        for pair in range(4):
            at = zlo * 1024 + pair * 256
            one = hidden_ref[:, at : at + 128].astype(F32)
            two = hidden_ref[:, at + 128 : at + 256].astype(F32)
            to = slice(pair * 128, pair * 128 + 128)
            even = jnp.where(low, one, pltpu.roll(two, 64, 1)).astype(BF16)
            odd = jnp.where(low, pltpu.roll(one, 64, 1), two).astype(BF16)
            hidden_out[TOKENS_ORDER.index(zlo), :, to] = even
            hidden_out[TOKENS_ORDER.index(8 + zlo), :, to] = odd


def prepare(hidden, queries):
    return pl.pallas_call(
        prepare_kernel,
        out_shape=(
            jax.ShapeDtypeStruct((16, STEPS, 512), BF16),
            jax.ShapeDtypeStruct((OWN_ROWS, HD), BF16),
        ),
        in_specs=[HBM, HBM],
        out_specs=(VMEM, VMEM),
        scratch_shapes=[
            pltpu.VMEM((OWN_ROWS, HD), F32),
            pltpu.VMEM(hidden.shape, BF16),
            pltpu.VMEM(queries.shape, BF16),
            pltpu.SemaphoreType.DMA((2,)),
        ],
        compiler_params=PARAMS,
        cost_estimate=pl.CostEstimate(flops=1 << 16, bytes_accessed=1 << 18, transcendentals=0),
        name="prepare",
    )(in_hbm(hidden), in_hbm(queries))


ORDER = (0, 1, 3, 2)


def fetch_kernel(keys_hbm, values_hbm, keys_ref, values_ref, sems):
    copies = (
        pltpu.make_async_copy(keys_hbm, keys_ref, sems.at[0]),
        pltpu.make_async_copy(values_hbm, values_ref, sems.at[1]),
    )
    for copy in copies:
        copy.start()
    for copy in copies:
        copy.wait()


def fetch(keys, values):
    return pl.pallas_call(
        fetch_kernel,
        out_shape=(pltpu.VMEM(keys.shape, BF16), pltpu.VMEM(values.shape, BF16)),
        in_specs=[HBM, HBM],
        out_specs=(VMEM, VMEM),
        scratch_shapes=[pltpu.SemaphoreType.DMA((2,))],
        compiler_params=PARAMS,
        cost_estimate=pl.CostEstimate(flops=1, bytes_accessed=1, transcendentals=0),
        name="fetch",
    )(in_hbm(keys), in_hbm(values))


def attend_kernel(
    lengths_ref,
    near_ref,
    far_ref,
    keys_ref,
    values_ref,
    kept_ref,
    sent_ref,
    spread,
):
    tensor = lax.axis_index("tensor")
    spread[...] = jnp.zeros_like(spread)
    starts = []
    for k in range(TENSOR):
        start = (tensor ^ ORDER[k]) * (LOCAL_HEADS * HD)
        starts.append(start)
        for head in range(LOCAL_HEADS):
            lanes = pl.ds(pl.multiple_of(start + head * HD, HD), HD)
            at = (k % 2) * OWN_ROWS + head * HEAD_ROWS
            to = k * OWN_ROWS + head * HEAD_ROWS
            piece = (near_ref, far_ref)[k // 2][at : at + HEAD_ROWS, :]
            spread[to : to + HEAD_ROWS, lanes] = piece
    scores = lax.dot_general(
        keys_ref[0], spread[...], (((1,), (1,)), ((), ())), preferred_element_type=F32
    ) * (HD**-0.5)
    held = scores.shape[0]
    position = tensor * held + lax.broadcasted_iota(jnp.int32, scores.shape, 0)
    allowed = position < lengths_ref[...]
    masked = jnp.where(allowed, scores, NEG_FILL)
    maxima = jnp.max(masked, axis=0, keepdims=True)
    weights = jnp.where(allowed, jnp.exp(masked - maxima), 0.0)
    totals = jnp.sum(weights, axis=0, keepdims=True)
    rounded = weights.astype(BF16)
    for half, out_ref in enumerate((kept_ref, sent_ref)):
        span = slice(half * 128, half * 128 + 128)
        values = jnp.concatenate(
            [
                values_ref[0, :, pl.ds(pl.multiple_of(starts[2 * half + n], 256), 256)]
                for n in range(2)
            ],
            axis=1,
        )
        summed = lax.dot_general(
            rounded[:, span], values, (((0,), (0,)), ((), ())), preferred_element_type=F32
        )
        pair = jnp.concatenate([maxima[:, span], totals[:, span]], axis=0)
        for n in range(2):
            for head in range(LOCAL_HEADS):
                at = n * LOCAL_HEADS + head
                out_ref[n, head * HEAD_ROWS : (head + 1) * HEAD_ROWS, :] = summed[
                    at * HEAD_ROWS : (at + 1) * HEAD_ROWS, at * HD : (at + 1) * HD
                ]
            out_ref[n, OWN_ROWS : OWN_ROWS + 2, :] = pltpu.roll(pair, 64, 1) if n else pair


def attend(lengths, near, far, keys, values):
    return pl.pallas_call(
        attend_kernel,
        out_shape=(jax.ShapeDtypeStruct((2, OWN_ROWS + 8, HD), F32),) * 2,
        in_specs=[VMEM] * 5,
        out_specs=(VMEM, VMEM),
        scratch_shapes=[pltpu.VMEM((KVH * HEAD_ROWS, KVH * HD), BF16)],
        compiler_params=PARAMS,
        cost_estimate=pl.CostEstimate(flops=1, bytes_accessed=1, transcendentals=0),
        name="attend",
    )(lengths, near, far, keys, values)


def merge_kernel(kept_ref, come_ref, own_ref, next_ref):
    rows = []
    for n in range(2):
        stats = [ref[n, OWN_ROWS : OWN_ROWS + 2, :] for ref in (kept_ref, come_ref)]
        joined = jnp.maximum(stats[0][:1], stats[1][:1])
        scales = [jnp.exp(stat[:1] - joined) for stat in stats]
        total = stats[0][1:] * scales[0] + stats[1][1:] * scales[1]
        out_ref = (own_ref, next_ref)[n]
        out_ref[OWN_ROWS : OWN_ROWS + 2, :] = jnp.concatenate([joined, total], axis=0)
        rows += scales
    columns = jnp.transpose(jnp.concatenate(rows + rows, axis=0), (1, 0))
    for n in range(2):
        out_ref = (own_ref, next_ref)[n]
        out_ref[:OWN_ROWS, :] = (
            kept_ref[n, :OWN_ROWS, :] * columns[:OWN_ROWS, 2 * n : 2 * n + 1]
            + come_ref[n, :OWN_ROWS, :] * columns[:OWN_ROWS, 2 * n + 1 : 2 * n + 2]
        )


def merge(kept, come):
    return pl.pallas_call(
        merge_kernel,
        out_shape=(jax.ShapeDtypeStruct((OWN_ROWS + 8, HD), F32),) * 2,
        in_specs=[VMEM, VMEM],
        out_specs=(VMEM, VMEM),
        compiler_params=PARAMS,
        cost_estimate=pl.CostEstimate(
            flops=1 << 17, bytes_accessed=1 << 18, transcendentals=1 << 9
        ),
        name="merge",
    )(kept, come)


def project_kernel(hidden_ref, own_ref, other_ref, out_ref, tokens):
    core = lax.axis_index("core")
    x = lax.axis_index("x")
    odd = x % 2 == 1
    for z in range(16):
        tokens[z * STEPS : (z + 1) * STEPS, :] = hidden_ref[z].astype(F32)
    partial = jnp.zeros((16 * STEPS, 512), F32)
    for swap, weight_ref in enumerate((own_ref, other_ref)):
        for pair in range(2):
            at = (core ^ swap) * 256 + ((x // 2) ^ pair) * 128
            block = tokens[:, pl.ds(pl.multiple_of(at, 128), 128)]
            turned = pltpu.roll(block, 64, 1)
            block = jnp.where(odd, *((block, turned) if pair else (turned, block)))
            partial += jnp.dot(
                block.astype(BF16),
                weight_ref[pair * 128 : pair * 128 + 128, :],
                preferred_element_type=F32,
            )
    for z in range(16):
        at = TOKENS_ORDER.index(z) * STEPS
        out_ref[SUMS_ORDER.index(z)] = partial[at : at + STEPS, :]


def project(hidden, own, other):
    return pl.pallas_call(
        project_kernel,
        out_shape=jax.ShapeDtypeStruct((16, STEPS, 512), F32),
        in_specs=[VMEM, VMEM, VMEM],
        out_specs=VMEM,
        scratch_shapes=[pltpu.VMEM((64, 512), F32)],
        compiler_params=PARAMS,
        cost_estimate=pl.CostEstimate(
            flops=2 * 64 * 512 * 512, bytes_accessed=1 << 20, transcendentals=0
        ),
        name="project",
    )(hidden, own, other)


def finish_kernel(
    part0_ref,
    part1_ref,
    sums_ref,
    queries_ref,
    cos_ref,
    sin_ref,
    attended_ref,
    keys_ref,
    values_ref,
    wide,
):
    parts = (part0_ref, part1_ref)
    projected = jnp.sum(sums_ref[...], axis=0)
    cos_part = cos_ref[...]
    sin_part = sin_ref[...]
    new_values = projected[:, LOCAL_HEADS * HD :].astype(BF16)
    values_ref[...] = new_values
    queries = queries_ref[:OWN_ROWS]
    fresh = []
    for head in range(LOCAL_HEADS):
        front = projected[:, head * HD : (head + 1) * HD]
        turned = (front * cos_part + pltpu.roll(front, HD // 2, 1) * sin_part).astype(BF16)
        keys_ref[:, head * HD : (head + 1) * HD] = turned
        fresh.append(
            lax.dot_general(
                turned, queries, (((1,), (1,)), ((), ())), preferred_element_type=F32
            )
        )
    lane = lane_iota((STEPS, OWN_ROWS))
    scores = jnp.where(lane < HEAD_ROWS, fresh[0], fresh[1]) * (HD**-0.5)
    step = (lane % HEAD_ROWS) // GROUP
    allowed = lax.broadcasted_iota(jnp.int32, (STEPS, OWN_ROWS), 0) <= step
    masked = jnp.where(allowed, scores, NEG_FILL)
    maxima = [part[OWN_ROWS : OWN_ROWS + 1, :OWN_ROWS] for part in parts]
    joined = jnp.max(masked, axis=0, keepdims=True)
    for part in maxima:
        joined = jnp.maximum(joined, part)
    weights = jnp.where(allowed, jnp.exp(masked - joined), 0.0)
    totals = jnp.sum(weights, axis=0, keepdims=True)
    scales = []
    for t in range(len(parts)):
        scale = jnp.exp(maxima[t] - joined)
        totals += parts[t][OWN_ROWS + 1 : OWN_ROWS + 2, :OWN_ROWS] * scale
        scales.append(scale)
    factors = jnp.concatenate([*scales, weights.astype(BF16).astype(F32)], axis=0) / totals
    factors = jnp.concatenate([factors, jnp.zeros((6, 128 - OWN_ROWS), F32)], axis=1)
    factors = jnp.concatenate([factors, jnp.zeros((2, 128), F32)], axis=0)
    columns = jnp.transpose(factors, (1, 0))
    values = new_values.astype(F32)
    for head in range(LOCAL_HEADS):
        rows = slice(head * HEAD_ROWS, (head + 1) * HEAD_ROWS)
        total = jnp.zeros((HEAD_ROWS, HD), F32)
        for t in range(len(parts)):
            total += parts[t][rows, :] * columns[rows, t : t + 1]
        for t in range(STEPS):
            total += columns[rows, 2 + t : 3 + t] * values[t : t + 1, head * HD : (head + 1) * HD]
        for s in range(STEPS):
            for member in range(GROUP):
                at = (head * GROUP + member) * HD
                row = s * GROUP + member
                wide[s : s + 1, at : at + HD] = total[row : row + 1, :]
    attended_ref[...] = wide[...].astype(BF16)


def finish(parts, sums, queries, cos_part, sin_part):
    return pl.pallas_call(
        finish_kernel,
        out_shape=(
            jax.ShapeDtypeStruct((STEPS, LOCAL_HEADS * GROUP * HD), BF16),
            jax.ShapeDtypeStruct((STEPS, LOCAL_HEADS * HD), BF16),
            jax.ShapeDtypeStruct((STEPS, LOCAL_HEADS * HD), BF16),
        ),
        in_specs=[VMEM] * 6,
        out_specs=(VMEM,) * 3,
        scratch_shapes=[pltpu.VMEM((STEPS, LOCAL_HEADS * GROUP * HD), F32)],
        compiler_params=PARAMS,
        cost_estimate=pl.CostEstimate(
            flops=1 << 20, bytes_accessed=1 << 19, transcendentals=1 << 10
        ),
        name="finish",
    )(*parts, sums, queries, cos_part, sin_part)


def rotation(lengths):
    half = HD // 2
    positions = lengths[None, :] + jnp.arange(STEPS, dtype=jnp.int32)[:, None]
    frequency = ROPE_BASE ** (-jnp.arange(half, dtype=F32) * 2.0 / HD)
    phases = positions.astype(F32) * frequency[None, :]
    cos_part = jnp.cos(phases)
    sin_part = jnp.sin(phases)
    return (
        jnp.concatenate([cos_part, cos_part], axis=-1),
        jnp.concatenate([-sin_part, sin_part], axis=-1),
    )


def exchange_z(blocks, order):
    return lax.all_to_all(blocks, Z_AXES, 0, 0, axis_index_groups=[order])


def with_partner(values, axis, flip, size=4):
    return lax.ppermute(values, axis, [(i, i ^ flip) for i in range(size)])


def body(hidden, kv_weight, queries, key_cache, value_cache, lengths):
    weight = kv_weight.reshape(64, 512)
    chunks, own_queries = prepare(
        gate(hidden.reshape(STEPS, -1), weight), queries.reshape(STEPS, -1)
    )
    come = with_partner(weight, "x", 1)
    weight = jnp.concatenate([weight, come], axis=0)
    near = jnp.concatenate([own_queries, with_partner(own_queries, "tensor", 1)], axis=0)
    tokens = exchange_z(gate(chunks, come), TOKENS_ORDER)
    far = with_partner(near, "tensor", 3)
    weight = jnp.concatenate([weight, with_partner(weight, "x", 3)], axis=0)
    keys, values = fetch(gate(key_cache, weight), value_cache)
    kept, sent = attend(jnp.broadcast_to(lengths, (1, KVH * HEAD_ROWS)), near, far, keys, values)
    other = with_partner(gate(weight, tokens, far, keys), "core", 1, 2)
    partial = project(tokens, weight, gate(other, kept))
    sums = exchange_z(partial, SUMS_ORDER)
    own_part, next_part = merge(kept, with_partner(sent, "tensor", 3))
    parts = (own_part, with_partner(next_part, "tensor", 1))
    cos_part, sin_part = rotation(lengths)
    outs = finish(parts, sums, near, cos_part, sin_part)
    return tuple(out.reshape(STEPS, 1, -1) for out in outs)


def solution(mesh):
    split = Mesh(mesh.devices.reshape(8, 2, 4, 4, 2), ("zlo", "core", "tensor", "x", "zhi"))
    return jax.shard_map(
        body,
        mesh=split,
        in_specs=(
            P(None, ROWS_AXES, None),
            P(ROWS_AXES, None, "tensor"),
            P(None, ROWS_AXES, "tensor"),
            P(ROWS_AXES, "tensor", None),
            P(ROWS_AXES, "tensor", None),
            P(ROWS_AXES),
        ),
        out_specs=(
            P(None, ROWS_AXES, "tensor"),
            P(None, ROWS_AXES, "tensor"),
            P(None, ROWS_AXES, "tensor"),
        ),
        check_vma=False,
    )
```

```python
import jax
import jax.numpy as jnp
from jax import lax
from jax.experimental import pallas as pl
from jax.experimental.pallas import tpu as pltpu
from jax.sharding import Mesh
from jax.sharding import PartitionSpec as P

KVH = 8
HQ = 64
HD = 128
STEPS = 4
GROUP = HQ // KVH
TENSOR = 4
LOCAL_HEADS = KVH // TENSOR
HEAD_ROWS = STEPS * GROUP
OWN_ROWS = LOCAL_HEADS * HEAD_ROWS
WIDTH = LOCAL_HEADS * HD
ROPE_BASE = 500000.0
NEG_FILL = -1e30
F32 = jnp.float32
BF16 = jnp.bfloat16
PARAMS = pltpu.CompilerParams(vmem_limit_bytes=16 * 1024 * 1024)
ROWS_AXES = ("zlo", "core", "x", "zhi")
Z_AXES = ("zhi", "zlo")
def ring(first):
    return [(first + hops) % 16 for hops in range(16)]


TOKENS_ORDER = ring(11)
SUMS_ORDER = ring(0)


def lane_iota(shape):
    return lax.broadcasted_iota(jnp.int32, shape, 1)


SMEM = pl.BlockSpec(memory_space=pltpu.SMEM)
VMEM = pl.BlockSpec(memory_space=pltpu.VMEM)
HBM = pl.BlockSpec(memory_space=pltpu.HBM)


def gate(values, *after):
    return lax.optimization_barrier((values, *after))[0]


def in_hbm(array):
    return pltpu.with_memory_space_constraint(array, pltpu.HBM)


def prepare_kernel(
    hidden_hbm, queries_hbm, hidden_out, queries_out, rows, hidden_ref, queries_ref, sems
):
    query_copy = pltpu.make_async_copy(queries_hbm, queries_ref, sems.at[0])
    hidden_copy = pltpu.make_async_copy(hidden_hbm, hidden_ref, sems.at[1])
    query_copy.start()
    hidden_copy.start()
    query_copy.wait()
    for head in range(LOCAL_HEADS):
        for member in range(GROUP):
            at = (head * GROUP + member) * HD
            piece = queries_ref[:, at : at + HD].astype(F32)
            for step in range(STEPS):
                row = head * HEAD_ROWS + step * GROUP + member
                rows[row : row + 1, :] = piece[step : step + 1, :]
    queries_out[...] = rows[...].astype(BF16)
    hidden_copy.wait()
    low = lane_iota((STEPS, 128)) < 64
    for zlo in range(8):
        for pair in range(4):
            at = zlo * 1024 + pair * 256
            one = hidden_ref[:, at : at + 128].astype(F32)
            two = hidden_ref[:, at + 128 : at + 256].astype(F32)
            to = slice(pair * 128, pair * 128 + 128)
            even = jnp.where(low, one, pltpu.roll(two, 64, 1)).astype(BF16)
            odd = jnp.where(low, pltpu.roll(one, 64, 1), two).astype(BF16)
            hidden_out[TOKENS_ORDER.index(zlo), :, to] = even
            hidden_out[TOKENS_ORDER.index(8 + zlo), :, to] = odd


def prepare(hidden, queries):
    return pl.pallas_call(
        prepare_kernel,
        out_shape=(
            jax.ShapeDtypeStruct((16, STEPS, 512), BF16),
            jax.ShapeDtypeStruct((OWN_ROWS, HD), BF16),
        ),
        in_specs=[HBM, HBM],
        out_specs=(VMEM, VMEM),
        scratch_shapes=[
            pltpu.VMEM((OWN_ROWS, HD), F32),
            pltpu.VMEM(hidden.shape, BF16),
            pltpu.VMEM(queries.shape, BF16),
            pltpu.SemaphoreType.DMA((2,)),
        ],
        compiler_params=PARAMS,
        cost_estimate=pl.CostEstimate(flops=1 << 16, bytes_accessed=1 << 18, transcendentals=0),
        name="prepare",
    )(in_hbm(hidden), in_hbm(queries))


ORDER = (0, 1, 3, 2)


PART = (OWN_ROWS + 8, HD)
PACKED = (OWN_ROWS + 16, HD)


def store_part(ref, summed, stat):
    ref[:OWN_ROWS, :] = summed
    ref[OWN_ROWS : OWN_ROWS + 1, :] = stat


def pack_part(ref, summed, stat):
    ref[:OWN_ROWS, :] = summed.astype(BF16)
    terms = []
    for _ in range(3):
        terms.append(stat.astype(BF16).astype(F32))
        stat = stat - terms[-1]
    rest = jnp.zeros((PACKED[0] - OWN_ROWS - 3, HD), F32)
    ref[OWN_ROWS:, :] = jnp.concatenate([*terms, rest], axis=0).astype(BF16)


def load_part(ref):
    return ref[:OWN_ROWS, :], ref[OWN_ROWS : OWN_ROWS + 1, :]


def unpack_part(ref):
    stat = jnp.sum(ref[OWN_ROWS:, :].astype(F32), axis=0, keepdims=True)
    return ref[:OWN_ROWS, :].astype(F32), stat


def fetch_kernel(keys_hbm, values_hbm, keys_ref, values_ref, sems):
    copies = (
        pltpu.make_async_copy(keys_hbm, keys_ref, sems.at[0]),
        pltpu.make_async_copy(values_hbm, values_ref, sems.at[1]),
    )
    for copy in copies:
        copy.start()
    for copy in copies:
        copy.wait()


def fetch(keys, values):
    return pl.pallas_call(
        fetch_kernel,
        out_shape=(pltpu.VMEM(keys.shape, BF16), pltpu.VMEM(values.shape, BF16)),
        in_specs=[HBM, HBM],
        out_specs=(VMEM, VMEM),
        scratch_shapes=[pltpu.SemaphoreType.DMA((2,))],
        compiler_params=PARAMS,
        cost_estimate=pl.CostEstimate(flops=1, bytes_accessed=1, transcendentals=0),
        name="fetch",
    )(in_hbm(keys), in_hbm(values))


def attend_kernel(
    lengths_ref,
    near_ref,
    far_ref,
    keys_ref,
    values_ref,
    kept_ref,
    sent_ref,
    spread,
):
    tensor = lax.axis_index("tensor")
    spread[...] = jnp.zeros_like(spread)
    starts = []
    for k in range(TENSOR):
        start = (tensor ^ ORDER[k]) * (LOCAL_HEADS * HD)
        starts.append(start)
        for head in range(LOCAL_HEADS):
            lanes = pl.ds(pl.multiple_of(start + head * HD, HD), HD)
            at = (k % 2) * OWN_ROWS + head * HEAD_ROWS
            to = k * OWN_ROWS + head * HEAD_ROWS
            piece = (near_ref, far_ref)[k // 2][at : at + HEAD_ROWS, :]
            spread[to : to + HEAD_ROWS, lanes] = piece
    scores = lax.dot_general(
        keys_ref[0], spread[...], (((1,), (1,)), ((), ())), preferred_element_type=F32
    ) * (HD**-0.5)
    held = scores.shape[0]
    position = tensor * held + lax.broadcasted_iota(jnp.int32, scores.shape, 0)
    allowed = position < lengths_ref[...]
    masked = jnp.where(allowed, scores, NEG_FILL)
    maxima = jnp.max(masked, axis=0, keepdims=True)
    weights = jnp.where(allowed, jnp.exp(masked - maxima), 0.0)
    totals = jnp.sum(weights, axis=0, keepdims=True)
    rounded = weights.astype(BF16)
    for half, out_ref in enumerate((kept_ref, sent_ref)):
        span = slice(half * 128, half * 128 + 128)
        values = jnp.concatenate(
            [
                values_ref[0, :, pl.ds(pl.multiple_of(starts[2 * half + n], 256), 256)]
                for n in range(2)
            ],
            axis=1,
        )
        summed = lax.dot_general(
            rounded[:, span], values, (((0,), (0,)), ((), ())), preferred_element_type=F32
        )
        low = lane_iota((1, 128)) < OWN_ROWS
        for n in range(2):
            blocks = []
            for head in range(LOCAL_HEADS):
                at = n * LOCAL_HEADS + head
                blocks.append(
                    summed[
                        at * HEAD_ROWS : (at + 1) * HEAD_ROWS, at * HD : (at + 1) * HD
                    ]
                )
            stats = (maxima[:, span], totals[:, span])
            turned = [pltpu.roll(stat, OWN_ROWS, 1) for stat in stats]
            stat = jnp.where(low, *((turned[0], stats[1]) if n else (stats[0], turned[1])))
            if half == 0:
                store_part(kept_ref.at[n], jnp.concatenate(blocks, axis=0), stat)
            else:
                pack_part(sent_ref.at[n], jnp.concatenate(blocks, axis=0), stat)


def attend(lengths, near, far, keys, values):
    return pl.pallas_call(
        attend_kernel,
        out_shape=(
            jax.ShapeDtypeStruct((2, *PART), F32),
            jax.ShapeDtypeStruct((2, *PACKED), BF16),
        ),
        in_specs=[VMEM] * 5,
        out_specs=(VMEM, VMEM),
        scratch_shapes=[pltpu.VMEM((KVH * HEAD_ROWS, KVH * HD), BF16)],
        compiler_params=PARAMS,
        cost_estimate=pl.CostEstimate(flops=1, bytes_accessed=1, transcendentals=0),
        name="attend",
    )(lengths, near, far, keys, values)


def merge_kernel(kept_ref, come_ref, own_ref, next_ref):
    low = lane_iota((1, 128)) < OWN_ROWS
    summed, rows, stats = [], [], []
    for n in range(2):
        parts = (load_part(kept_ref.at[n]), unpack_part(come_ref.at[n]))
        joined = jnp.maximum(parts[0][1], parts[1][1])
        scales = [jnp.exp(stat - joined) for _, stat in parts]
        total = sum(
            stat * pltpu.roll(scale, OWN_ROWS, 1) for (_, stat), scale in zip(parts, scales)
        )
        summed.append([part for part, _ in parts])
        rows += scales
        stats.append(jnp.where(low, joined, total))
    columns = jnp.transpose(jnp.concatenate(rows + rows, axis=0), (1, 0))
    merged = [
        summed[n][0] * columns[:OWN_ROWS, 2 * n : 2 * n + 1]
        + summed[n][1] * columns[:OWN_ROWS, 2 * n + 1 : 2 * n + 2]
        for n in range(2)
    ]
    store_part(own_ref, merged[0], stats[0])
    pack_part(next_ref, merged[1], stats[1])


def merge(kept, come):
    return pl.pallas_call(
        merge_kernel,
        out_shape=(jax.ShapeDtypeStruct(PART, F32), jax.ShapeDtypeStruct(PACKED, BF16)),
        in_specs=[VMEM, VMEM],
        out_specs=(VMEM, VMEM),
        compiler_params=PARAMS,
        cost_estimate=pl.CostEstimate(
            flops=1 << 17, bytes_accessed=1 << 18, transcendentals=1 << 9
        ),
        name="merge",
    )(kept, come)


def project_kernel(hidden_ref, own_ref, other_ref, out_ref, tokens):
    core = lax.axis_index("core")
    x = lax.axis_index("x")
    odd = x % 2 == 1
    for z in range(16):
        tokens[z * STEPS : (z + 1) * STEPS, :] = hidden_ref[z].astype(F32)
    partial = jnp.zeros((16 * STEPS, 512), F32)
    for swap, weight_ref in enumerate((own_ref, other_ref)):
        for pair in range(2):
            at = (core ^ swap) * 256 + ((x // 2) ^ pair) * 128
            block = tokens[:, pl.ds(pl.multiple_of(at, 128), 128)]
            turned = pltpu.roll(block, 64, 1)
            block = jnp.where(odd, *((block, turned) if pair else (turned, block)))
            partial += jnp.dot(
                block.astype(BF16),
                weight_ref[pair * 128 : pair * 128 + 128, :],
                preferred_element_type=F32,
            )
    leading = partial.astype(BF16).astype(F32)
    trailing = (partial - leading)[:, :WIDTH]
    for z in range(16):
        at = TOKENS_ORDER.index(z) * STEPS
        out_ref[SUMS_ORDER.index(z), :, : 2 * WIDTH] = leading[at : at + STEPS, :].astype(BF16)
        out_ref[SUMS_ORDER.index(z), :, 2 * WIDTH :] = trailing[at : at + STEPS, :].astype(BF16)


def project(hidden, own, other):
    return pl.pallas_call(
        project_kernel,
        out_shape=jax.ShapeDtypeStruct((16, STEPS, 3 * WIDTH), BF16),
        in_specs=[VMEM, VMEM, VMEM],
        out_specs=VMEM,
        scratch_shapes=[pltpu.VMEM((64, 512), F32)],
        compiler_params=PARAMS,
        cost_estimate=pl.CostEstimate(
            flops=2 * 64 * 512 * 512, bytes_accessed=1 << 20, transcendentals=0
        ),
        name="project",
    )(hidden, own, other)


def finish_kernel(
    part0_ref,
    part1_ref,
    sums_ref,
    queries_ref,
    cos_ref,
    sin_ref,
    attended_ref,
    keys_ref,
    values_ref,
    wide,
):
    parts = (load_part(part0_ref), unpack_part(part1_ref))
    projected = jnp.sum(sums_ref[...].astype(F32), axis=0)
    new_keys = projected[:, :WIDTH] + projected[:, 2 * WIDTH :]
    cos_part = cos_ref[...]
    sin_part = sin_ref[...]
    new_values = projected[:, WIDTH : 2 * WIDTH].astype(BF16)
    values_ref[...] = new_values
    queries = queries_ref[:OWN_ROWS]
    fresh = []
    for head in range(LOCAL_HEADS):
        front = new_keys[:, head * HD : (head + 1) * HD]
        turned = (front * cos_part + pltpu.roll(front, HD // 2, 1) * sin_part).astype(BF16)
        keys_ref[:, head * HD : (head + 1) * HD] = turned
        fresh.append(
            lax.dot_general(
                turned, queries, (((1,), (1,)), ((), ())), preferred_element_type=F32
            )
        )
    lane = lane_iota((STEPS, OWN_ROWS))
    scores = jnp.where(lane < HEAD_ROWS, fresh[0], fresh[1]) * (HD**-0.5)
    step = (lane % HEAD_ROWS) // GROUP
    allowed = lax.broadcasted_iota(jnp.int32, (STEPS, OWN_ROWS), 0) <= step
    masked = jnp.where(allowed, scores, NEG_FILL)
    maxima = [stat[:, :OWN_ROWS] for _, stat in parts]
    joined = jnp.max(masked, axis=0, keepdims=True)
    for part in maxima:
        joined = jnp.maximum(joined, part)
    weights = jnp.where(allowed, jnp.exp(masked - joined), 0.0)
    totals = jnp.sum(weights, axis=0, keepdims=True)
    scales = []
    for t in range(len(parts)):
        scale = jnp.exp(maxima[t] - joined)
        totals += pltpu.roll(parts[t][1], OWN_ROWS, 1)[:, :OWN_ROWS] * scale
        scales.append(scale)
    factors = jnp.concatenate([*scales, weights.astype(BF16).astype(F32)], axis=0) / totals
    factors = jnp.concatenate([factors, jnp.zeros((6, 128 - OWN_ROWS), F32)], axis=1)
    factors = jnp.concatenate([factors, jnp.zeros((2, 128), F32)], axis=0)
    columns = jnp.transpose(factors, (1, 0))
    values = new_values.astype(F32)
    for head in range(LOCAL_HEADS):
        rows = slice(head * HEAD_ROWS, (head + 1) * HEAD_ROWS)
        total = jnp.zeros((HEAD_ROWS, HD), F32)
        for t in range(len(parts)):
            total += parts[t][0][rows, :] * columns[rows, t : t + 1]
        for t in range(STEPS):
            total += columns[rows, 2 + t : 3 + t] * values[t : t + 1, head * HD : (head + 1) * HD]
        for s in range(STEPS):
            for member in range(GROUP):
                at = (head * GROUP + member) * HD
                row = s * GROUP + member
                wide[s : s + 1, at : at + HD] = total[row : row + 1, :]
    attended_ref[...] = wide[...].astype(BF16)


def finish(parts, sums, queries, cos_part, sin_part):
    return pl.pallas_call(
        finish_kernel,
        out_shape=(
            jax.ShapeDtypeStruct((STEPS, LOCAL_HEADS * GROUP * HD), BF16),
            jax.ShapeDtypeStruct((STEPS, LOCAL_HEADS * HD), BF16),
            jax.ShapeDtypeStruct((STEPS, LOCAL_HEADS * HD), BF16),
        ),
        in_specs=[VMEM] * 6,
        out_specs=(VMEM,) * 3,
        scratch_shapes=[pltpu.VMEM((STEPS, LOCAL_HEADS * GROUP * HD), F32)],
        compiler_params=PARAMS,
        cost_estimate=pl.CostEstimate(
            flops=1 << 20, bytes_accessed=1 << 19, transcendentals=1 << 10
        ),
        name="finish",
    )(*parts, sums, queries, cos_part, sin_part)


def rotation(lengths):
    half = HD // 2
    positions = lengths[None, :] + jnp.arange(STEPS, dtype=jnp.int32)[:, None]
    frequency = ROPE_BASE ** (-jnp.arange(half, dtype=F32) * 2.0 / HD)
    phases = positions.astype(F32) * frequency[None, :]
    cos_part = jnp.cos(phases)
    sin_part = jnp.sin(phases)
    return (
        jnp.concatenate([cos_part, cos_part], axis=-1),
        jnp.concatenate([-sin_part, sin_part], axis=-1),
    )


def exchange_z(blocks, order):
    return lax.all_to_all(blocks, Z_AXES, 0, 0, axis_index_groups=[order])


def with_partner(values, axis, flip, size=4):
    return lax.ppermute(values, axis, [(i, i ^ flip) for i in range(size)])


def body(hidden, kv_weight, queries, key_cache, value_cache, lengths):
    weight = kv_weight.reshape(64, 512)
    chunks, own_queries = prepare(
        gate(hidden.reshape(STEPS, -1), weight), queries.reshape(STEPS, -1)
    )
    come = with_partner(weight, "x", 1)
    weight = jnp.concatenate([weight, come], axis=0)
    near = jnp.concatenate([own_queries, with_partner(own_queries, "tensor", 1)], axis=0)
    tokens = exchange_z(gate(chunks, come), TOKENS_ORDER)
    far = with_partner(near, "tensor", 3)
    weight = jnp.concatenate([weight, with_partner(weight, "x", 3)], axis=0)
    keys, values = fetch(gate(key_cache, weight), value_cache)
    kept, sent = attend(jnp.broadcast_to(lengths, (1, KVH * HEAD_ROWS)), near, far, keys, values)
    other = with_partner(gate(weight, tokens, far, keys), "core", 1, 2)
    partial = project(tokens, weight, gate(other, kept))
    sums = exchange_z(partial, SUMS_ORDER)
    own_part, next_part = merge(kept, with_partner(sent, "tensor", 3))
    parts = (own_part, with_partner(next_part, "tensor", 1))
    cos_part, sin_part = rotation(lengths)
    outs = finish(parts, sums, near, cos_part, sin_part)
    return tuple(out.reshape(STEPS, 1, -1) for out in outs)


def solution(mesh):
    split = Mesh(mesh.devices.reshape(8, 2, 4, 4, 2), ("zlo", "core", "tensor", "x", "zhi"))
    return jax.shard_map(
        body,
        mesh=split,
        in_specs=(
            P(None, ROWS_AXES, None),
            P(ROWS_AXES, None, "tensor"),
            P(None, ROWS_AXES, "tensor"),
            P(ROWS_AXES, "tensor", None),
            P(ROWS_AXES, "tensor", None),
            P(ROWS_AXES),
        ),
        out_specs=(
            P(None, ROWS_AXES, "tensor"),
            P(None, ROWS_AXES, "tensor"),
            P(None, ROWS_AXES, "tensor"),
        ),
        check_vma=False,
    )
```

```python
import jax
import jax.numpy as jnp
from jax import lax
from jax.experimental import pallas as pl
from jax.experimental.pallas import tpu as pltpu
from jax.sharding import Mesh
from jax.sharding import PartitionSpec as P

KVH = 8
HQ = 64
HD = 128
STEPS = 4
GROUP = HQ // KVH
TENSOR = 4
LOCAL_HEADS = KVH // TENSOR
HEAD_ROWS = STEPS * GROUP
OWN_ROWS = LOCAL_HEADS * HEAD_ROWS
WIDTH = LOCAL_HEADS * HD
ROPE_BASE = 500000.0
NEG_FILL = -1e30
F32 = jnp.float32
BF16 = jnp.bfloat16
PARAMS = pltpu.CompilerParams(vmem_limit_bytes=16 * 1024 * 1024)
ROWS_AXES = ("zlo", "core", "x", "zhi")
Z_AXES = ("zhi", "zlo")
def ring(first):
    return [(first + hops) % 16 for hops in range(16)]


TOKENS_ORDER = ring(11)
SUMS_ORDER = ring(0)


def lane_iota(shape):
    return lax.broadcasted_iota(jnp.int32, shape, 1)


SMEM = pl.BlockSpec(memory_space=pltpu.SMEM)
VMEM = pl.BlockSpec(memory_space=pltpu.VMEM)
HBM = pl.BlockSpec(memory_space=pltpu.HBM)


def gate(values, *after):
    return lax.optimization_barrier((values, *after))[0]


def in_hbm(array):
    return pltpu.with_memory_space_constraint(array, pltpu.HBM)


def prepare_kernel(
    hidden_hbm, queries_hbm, hidden_out, queries_out, rows, hidden_ref, queries_ref, sems
):
    query_copy = pltpu.make_async_copy(queries_hbm, queries_ref, sems.at[0])
    hidden_copy = pltpu.make_async_copy(hidden_hbm, hidden_ref, sems.at[1])
    query_copy.start()
    hidden_copy.start()
    query_copy.wait()
    for head in range(LOCAL_HEADS):
        for member in range(GROUP):
            at = (head * GROUP + member) * HD
            piece = queries_ref[:, at : at + HD].astype(F32)
            for step in range(STEPS):
                row = head * HEAD_ROWS + step * GROUP + member
                rows[row : row + 1, :] = piece[step : step + 1, :]
    queries_out[...] = rows[...].astype(BF16)
    hidden_copy.wait()
    low = lane_iota((STEPS, 128)) < 64
    for zlo in range(8):
        for pair in range(4):
            at = zlo * 1024 + pair * 256
            one = hidden_ref[:, at : at + 128].astype(F32)
            two = hidden_ref[:, at + 128 : at + 256].astype(F32)
            to = slice(pair * 128, pair * 128 + 128)
            even = jnp.where(low, one, pltpu.roll(two, 64, 1)).astype(BF16)
            odd = jnp.where(low, pltpu.roll(one, 64, 1), two).astype(BF16)
            hidden_out[TOKENS_ORDER.index(zlo), :, to] = even
            hidden_out[TOKENS_ORDER.index(8 + zlo), :, to] = odd


def prepare(hidden, queries):
    return pl.pallas_call(
        prepare_kernel,
        out_shape=(
            jax.ShapeDtypeStruct((16, STEPS, 512), BF16),
            jax.ShapeDtypeStruct((OWN_ROWS, HD), BF16),
        ),
        in_specs=[HBM, HBM],
        out_specs=(VMEM, VMEM),
        scratch_shapes=[
            pltpu.VMEM((OWN_ROWS, HD), F32),
            pltpu.VMEM(hidden.shape, BF16),
            pltpu.VMEM(queries.shape, BF16),
            pltpu.SemaphoreType.DMA((2,)),
        ],
        compiler_params=PARAMS,
        cost_estimate=pl.CostEstimate(flops=1 << 16, bytes_accessed=1 << 18, transcendentals=0),
        name="prepare",
    )(in_hbm(hidden), in_hbm(queries))


ORDER = (0, 1, 3, 2)


PART = (OWN_ROWS + 8, HD)
PACKED = (OWN_ROWS + 16, HD)


def store_part(ref, summed, stat):
    ref[:OWN_ROWS, :] = summed
    ref[OWN_ROWS : OWN_ROWS + 1, :] = stat


def pack_part(ref, summed, stat):
    ref[:OWN_ROWS, :] = summed.astype(BF16)
    terms = []
    for _ in range(3):
        terms.append(stat.astype(BF16).astype(F32))
        stat = stat - terms[-1]
    rest = jnp.zeros((PACKED[0] - OWN_ROWS - 3, HD), F32)
    ref[OWN_ROWS:, :] = jnp.concatenate([*terms, rest], axis=0).astype(BF16)


def load_part(ref):
    return ref[:OWN_ROWS, :], ref[OWN_ROWS : OWN_ROWS + 1, :]


def unpack_part(ref):
    stat = jnp.sum(ref[OWN_ROWS:, :].astype(F32), axis=0, keepdims=True)
    return ref[:OWN_ROWS, :].astype(F32), stat


def fetch_kernel(keys_hbm, values_hbm, keys_ref, values_ref, sems):
    copies = (
        pltpu.make_async_copy(keys_hbm, keys_ref, sems.at[0]),
        pltpu.make_async_copy(values_hbm, values_ref, sems.at[1]),
    )
    for copy in copies:
        copy.start()
    for copy in copies:
        copy.wait()


def fetch(keys, values):
    return pl.pallas_call(
        fetch_kernel,
        out_shape=(pltpu.VMEM(keys.shape, BF16), pltpu.VMEM(values.shape, BF16)),
        in_specs=[HBM, HBM],
        out_specs=(VMEM, VMEM),
        scratch_shapes=[pltpu.SemaphoreType.DMA((2,))],
        compiler_params=PARAMS,
        cost_estimate=pl.CostEstimate(flops=1, bytes_accessed=1, transcendentals=0),
        name="fetch",
    )(in_hbm(keys), in_hbm(values))


def attend_kernel(
    lengths_ref,
    near_ref,
    far_ref,
    keys_ref,
    values_ref,
    kept_ref,
    sent_ref,
    spread,
):
    tensor = lax.axis_index("tensor")
    spread[...] = jnp.zeros_like(spread)
    starts = []
    for k in range(TENSOR):
        start = (tensor ^ ORDER[k]) * (LOCAL_HEADS * HD)
        starts.append(start)
        for head in range(LOCAL_HEADS):
            lanes = pl.ds(pl.multiple_of(start + head * HD, HD), HD)
            at = (k % 2) * OWN_ROWS + head * HEAD_ROWS
            to = k * OWN_ROWS + head * HEAD_ROWS
            piece = (near_ref, far_ref)[k // 2][at : at + HEAD_ROWS, :]
            spread[to : to + HEAD_ROWS, lanes] = piece
    scores = lax.dot_general(
        keys_ref[0], spread[...], (((1,), (1,)), ((), ())), preferred_element_type=F32
    ) * (HD**-0.5)
    held = scores.shape[0]
    position = tensor * held + lax.broadcasted_iota(jnp.int32, scores.shape, 0)
    allowed = position < lengths_ref[...]
    masked = jnp.where(allowed, scores, NEG_FILL)
    maxima = jnp.max(masked, axis=0, keepdims=True)
    weights = jnp.where(allowed, jnp.exp(masked - maxima), 0.0)
    totals = jnp.sum(weights, axis=0, keepdims=True)
    rounded = weights.astype(BF16)
    for half, out_ref in enumerate((kept_ref, sent_ref)):
        span = slice(half * 128, half * 128 + 128)
        values = jnp.concatenate(
            [
                values_ref[0, :, pl.ds(pl.multiple_of(starts[2 * half + n], 256), 256)]
                for n in range(2)
            ],
            axis=1,
        )
        summed = lax.dot_general(
            rounded[:, span], values, (((0,), (0,)), ((), ())), preferred_element_type=F32
        )
        low = lane_iota((1, 128)) < OWN_ROWS
        for n in range(2):
            blocks = []
            for head in range(LOCAL_HEADS):
                at = n * LOCAL_HEADS + head
                blocks.append(
                    summed[
                        at * HEAD_ROWS : (at + 1) * HEAD_ROWS, at * HD : (at + 1) * HD
                    ]
                )
            stats = (maxima[:, span], totals[:, span])
            turned = [pltpu.roll(stat, OWN_ROWS, 1) for stat in stats]
            stat = jnp.where(low, *((turned[0], stats[1]) if n else (stats[0], turned[1])))
            if half == 0:
                store_part(kept_ref.at[n], jnp.concatenate(blocks, axis=0), stat)
            else:
                pack_part(sent_ref.at[n], jnp.concatenate(blocks, axis=0), stat)


def attend(lengths, near, far, keys, values):
    return pl.pallas_call(
        attend_kernel,
        out_shape=(
            jax.ShapeDtypeStruct((2, *PART), F32),
            jax.ShapeDtypeStruct((2, *PACKED), BF16),
        ),
        in_specs=[VMEM] * 5,
        out_specs=(VMEM, VMEM),
        scratch_shapes=[pltpu.VMEM((KVH * HEAD_ROWS, KVH * HD), BF16)],
        compiler_params=PARAMS,
        cost_estimate=pl.CostEstimate(flops=1, bytes_accessed=1, transcendentals=0),
        name="attend",
    )(lengths, near, far, keys, values)


def merge_kernel(kept_ref, come_ref, own_ref, next_ref):
    low = lane_iota((1, 128)) < OWN_ROWS
    summed, rows, stats = [], [], []
    for n in range(2):
        parts = (load_part(kept_ref.at[n]), unpack_part(come_ref.at[n]))
        joined = jnp.maximum(parts[0][1], parts[1][1])
        scales = [jnp.exp(stat - joined) for _, stat in parts]
        total = sum(
            stat * pltpu.roll(scale, OWN_ROWS, 1) for (_, stat), scale in zip(parts, scales)
        )
        summed.append([part for part, _ in parts])
        rows += scales
        stats.append(jnp.where(low, joined, total))
    columns = jnp.transpose(jnp.concatenate(rows + rows, axis=0), (1, 0))
    merged = [
        summed[n][0] * columns[:OWN_ROWS, 2 * n : 2 * n + 1]
        + summed[n][1] * columns[:OWN_ROWS, 2 * n + 1 : 2 * n + 2]
        for n in range(2)
    ]
    store_part(own_ref, merged[0], stats[0])
    pack_part(next_ref, merged[1], stats[1])


def merge(kept, come):
    return pl.pallas_call(
        merge_kernel,
        out_shape=(jax.ShapeDtypeStruct(PART, F32), jax.ShapeDtypeStruct(PACKED, BF16)),
        in_specs=[VMEM, VMEM],
        out_specs=(VMEM, VMEM),
        compiler_params=PARAMS,
        cost_estimate=pl.CostEstimate(
            flops=1 << 17, bytes_accessed=1 << 18, transcendentals=1 << 9
        ),
        name="merge",
    )(kept, come)


def project_kernel(hidden_ref, own_ref, other_ref, out_ref, tokens):
    core = lax.axis_index("core")
    x = lax.axis_index("x")
    odd = x % 2 == 1
    for z in range(16):
        tokens[z * STEPS : (z + 1) * STEPS, :] = hidden_ref[z].astype(F32)
    partial = jnp.zeros((16 * STEPS, 512), F32)
    for swap, weight_ref in enumerate((own_ref, other_ref)):
        for pair in range(2):
            at = (core ^ swap) * 256 + ((x // 2) ^ pair) * 128
            block = tokens[:, pl.ds(pl.multiple_of(at, 128), 128)]
            turned = pltpu.roll(block, 64, 1)
            block = jnp.where(odd, *((block, turned) if pair else (turned, block)))
            partial += jnp.dot(
                block.astype(BF16),
                weight_ref[pair * 128 : pair * 128 + 128, :],
                preferred_element_type=F32,
            )
    leading = partial.astype(BF16).astype(F32)
    trailing = (partial - leading)[:, :WIDTH]
    for z in range(16):
        at = TOKENS_ORDER.index(z) * STEPS
        out_ref[SUMS_ORDER.index(z), :, : 2 * WIDTH] = leading[at : at + STEPS, :].astype(BF16)
        out_ref[SUMS_ORDER.index(z), :, 2 * WIDTH :] = trailing[at : at + STEPS, :].astype(BF16)


def project(hidden, own, other):
    return pl.pallas_call(
        project_kernel,
        out_shape=jax.ShapeDtypeStruct((16, STEPS, 3 * WIDTH), BF16),
        in_specs=[VMEM, VMEM, VMEM],
        out_specs=VMEM,
        scratch_shapes=[pltpu.VMEM((64, 512), F32)],
        compiler_params=PARAMS,
        cost_estimate=pl.CostEstimate(
            flops=2 * 64 * 512 * 512, bytes_accessed=1 << 20, transcendentals=0
        ),
        name="project",
    )(hidden, own, other)


def finish_kernel(
    part0_ref,
    part1_ref,
    sums_ref,
    queries_ref,
    cos_ref,
    sin_ref,
    attended_ref,
    keys_ref,
    values_ref,
    wide,
):
    parts = (load_part(part0_ref), unpack_part(part1_ref))
    projected = jnp.sum(sums_ref[...].astype(F32), axis=0)
    new_keys = projected[:, :WIDTH] + projected[:, 2 * WIDTH :]
    cos_part = cos_ref[...]
    sin_part = sin_ref[...]
    new_values = projected[:, WIDTH : 2 * WIDTH].astype(BF16)
    values_ref[...] = new_values
    queries = queries_ref[:OWN_ROWS]
    fresh = []
    for head in range(LOCAL_HEADS):
        front = new_keys[:, head * HD : (head + 1) * HD]
        turned = (front * cos_part + pltpu.roll(front, HD // 2, 1) * sin_part).astype(BF16)
        keys_ref[:, head * HD : (head + 1) * HD] = turned
        fresh.append(
            lax.dot_general(
                turned, queries, (((1,), (1,)), ((), ())), preferred_element_type=F32
            )
        )
    lane = lane_iota((STEPS, OWN_ROWS))
    scores = jnp.where(lane < HEAD_ROWS, fresh[0], fresh[1]) * (HD**-0.5)
    step = (lane % HEAD_ROWS) // GROUP
    allowed = lax.broadcasted_iota(jnp.int32, (STEPS, OWN_ROWS), 0) <= step
    masked = jnp.where(allowed, scores, NEG_FILL)
    maxima = [stat[:, :OWN_ROWS] for _, stat in parts]
    joined = jnp.max(masked, axis=0, keepdims=True)
    for part in maxima:
        joined = jnp.maximum(joined, part)
    weights = jnp.where(allowed, jnp.exp(masked - joined), 0.0)
    totals = jnp.sum(weights, axis=0, keepdims=True)
    scales = []
    for t in range(len(parts)):
        scale = jnp.exp(maxima[t] - joined)
        totals += pltpu.roll(parts[t][1], OWN_ROWS, 1)[:, :OWN_ROWS] * scale
        scales.append(scale)
    factors = jnp.concatenate([*scales, weights.astype(BF16).astype(F32)], axis=0) / totals
    factors = jnp.concatenate([factors, jnp.zeros((6, 128 - OWN_ROWS), F32)], axis=1)
    factors = jnp.concatenate([factors, jnp.zeros((2, 128), F32)], axis=0)
    columns = jnp.transpose(factors, (1, 0))
    values = new_values.astype(F32)
    for head in range(LOCAL_HEADS):
        rows = slice(head * HEAD_ROWS, (head + 1) * HEAD_ROWS)
        total = jnp.zeros((HEAD_ROWS, HD), F32)
        for t in range(len(parts)):
            total += parts[t][0][rows, :] * columns[rows, t : t + 1]
        for t in range(STEPS):
            total += columns[rows, 2 + t : 3 + t] * values[t : t + 1, head * HD : (head + 1) * HD]
        for s in range(STEPS):
            for member in range(GROUP):
                at = (head * GROUP + member) * HD
                row = s * GROUP + member
                wide[s : s + 1, at : at + HD] = total[row : row + 1, :]
    attended_ref[...] = wide[...].astype(BF16)


def finish(parts, sums, queries, cos_part, sin_part):
    return pl.pallas_call(
        finish_kernel,
        out_shape=(
            jax.ShapeDtypeStruct((STEPS, LOCAL_HEADS * GROUP * HD), BF16),
            jax.ShapeDtypeStruct((STEPS, LOCAL_HEADS * HD), BF16),
            jax.ShapeDtypeStruct((STEPS, LOCAL_HEADS * HD), BF16),
        ),
        in_specs=[VMEM] * 6,
        out_specs=(VMEM,) * 3,
        scratch_shapes=[pltpu.VMEM((STEPS, LOCAL_HEADS * GROUP * HD), F32)],
        compiler_params=PARAMS,
        cost_estimate=pl.CostEstimate(
            flops=1 << 20, bytes_accessed=1 << 19, transcendentals=1 << 10
        ),
        name="finish",
    )(*parts, sums, queries, cos_part, sin_part)


def rotation(lengths):
    half = HD // 2
    positions = lengths[None, :] + jnp.arange(STEPS, dtype=jnp.int32)[:, None]
    frequency = ROPE_BASE ** (-jnp.arange(half, dtype=F32) * 2.0 / HD)
    phases = positions.astype(F32) * frequency[None, :]
    cos_part = jnp.cos(phases)
    sin_part = jnp.sin(phases)
    return (
        jnp.concatenate([cos_part, cos_part], axis=-1),
        jnp.concatenate([-sin_part, sin_part], axis=-1),
    )


def exchange_z(blocks, order):
    return lax.all_to_all(blocks, Z_AXES, 0, 0, axis_index_groups=[order])


def with_partner(values, axis, flip, size=4):
    return lax.ppermute(values, axis, [(i, i ^ flip) for i in range(size)])


def body(hidden, kv_weight, queries, key_cache, value_cache, lengths):
    weight = kv_weight.reshape(64, 512)
    chunks, own_queries = prepare(
        gate(hidden.reshape(STEPS, -1), weight), queries.reshape(STEPS, -1)
    )
    come = with_partner(weight, "x", 1)
    weight = jnp.concatenate([weight, come], axis=0)
    near = jnp.concatenate([own_queries, with_partner(own_queries, "tensor", 1)], axis=0)
    tokens = exchange_z(gate(chunks, come), TOKENS_ORDER)
    far = with_partner(near, "tensor", 3)
    weight = jnp.concatenate([weight, with_partner(weight, "x", 3)], axis=0)
    keys, values = fetch(gate(key_cache, weight), value_cache)
    kept, sent = attend(jnp.broadcast_to(lengths, (1, KVH * HEAD_ROWS)), near, far, keys, values)
    other = with_partner(weight, "core", 1, 2)
    partial = project(tokens, weight, gate(other, kept))
    sums = exchange_z(partial, SUMS_ORDER)
    own_part, next_part = merge(kept, with_partner(sent, "tensor", 3))
    parts = (own_part, with_partner(next_part, "tensor", 1))
    cos_part, sin_part = rotation(lengths)
    outs = finish(parts, sums, near, cos_part, sin_part)
    return tuple(out.reshape(STEPS, 1, -1) for out in outs)


def solution(mesh):
    split = Mesh(mesh.devices.reshape(8, 2, 4, 4, 2), ("zlo", "core", "tensor", "x", "zhi"))
    return jax.shard_map(
        body,
        mesh=split,
        in_specs=(
            P(None, ROWS_AXES, None),
            P(ROWS_AXES, None, "tensor"),
            P(None, ROWS_AXES, "tensor"),
            P(ROWS_AXES, "tensor", None),
            P(ROWS_AXES, "tensor", None),
            P(ROWS_AXES),
        ),
        out_specs=(
            P(None, ROWS_AXES, "tensor"),
            P(None, ROWS_AXES, "tensor"),
            P(None, ROWS_AXES, "tensor"),
        ),
        check_vma=False,
    )
```

```python
import jax
import jax.numpy as jnp
from jax import lax
from jax.experimental import pallas as pl
from jax.experimental.pallas import tpu as pltpu
from jax.sharding import Mesh
from jax.sharding import PartitionSpec as P

KVH = 8
HQ = 64
HD = 128
STEPS = 4
GROUP = HQ // KVH
TENSOR = 4
LOCAL_HEADS = KVH // TENSOR
HEAD_ROWS = STEPS * GROUP
OWN_ROWS = LOCAL_HEADS * HEAD_ROWS
WIDTH = LOCAL_HEADS * HD
ROPE_BASE = 500000.0
NEG_FILL = -1e30
F32 = jnp.float32
BF16 = jnp.bfloat16
PARAMS = pltpu.CompilerParams(vmem_limit_bytes=16 * 1024 * 1024)
ROWS_AXES = ("zlo", "core", "x", "zhi")
Z_AXES = ("zhi", "zlo")
def ring(first):
    return [(first + hops) % 16 for hops in range(16)]


TOKENS_ORDER = ring(11)
SUMS_ORDER = ring(0)


def lane_iota(shape):
    return lax.broadcasted_iota(jnp.int32, shape, 1)


SMEM = pl.BlockSpec(memory_space=pltpu.SMEM)
VMEM = pl.BlockSpec(memory_space=pltpu.VMEM)
HBM = pl.BlockSpec(memory_space=pltpu.HBM)


def gate(values, *after):
    return lax.optimization_barrier((values, *after))[0]


def in_hbm(array):
    return pltpu.with_memory_space_constraint(array, pltpu.HBM)


def prepare_kernel(hidden_ref, queries_ref, hidden_out, queries_out, rows):
    for head in range(LOCAL_HEADS):
        for member in range(GROUP):
            at = (head * GROUP + member) * HD
            piece = queries_ref[:, at : at + HD].astype(F32)
            for step in range(STEPS):
                row = head * HEAD_ROWS + step * GROUP + member
                rows[row : row + 1, :] = piece[step : step + 1, :]
    queries_out[...] = rows[...].astype(BF16)
    low = lane_iota((STEPS, 128)) < 64
    for zlo in range(8):
        for pair in range(4):
            at = zlo * 1024 + pair * 256
            one = hidden_ref[:, at : at + 128].astype(F32)
            two = hidden_ref[:, at + 128 : at + 256].astype(F32)
            to = slice(pair * 128, pair * 128 + 128)
            even = jnp.where(low, one, pltpu.roll(two, 64, 1)).astype(BF16)
            odd = jnp.where(low, pltpu.roll(one, 64, 1), two).astype(BF16)
            hidden_out[TOKENS_ORDER.index(zlo), :, to] = even
            hidden_out[TOKENS_ORDER.index(8 + zlo), :, to] = odd


def prepare(hidden, queries):
    return pl.pallas_call(
        prepare_kernel,
        out_shape=(
            jax.ShapeDtypeStruct((16, STEPS, 512), BF16),
            jax.ShapeDtypeStruct((OWN_ROWS, HD), BF16),
        ),
        in_specs=[VMEM, VMEM],
        out_specs=(VMEM, VMEM),
        scratch_shapes=[pltpu.VMEM((OWN_ROWS, HD), F32)],
        compiler_params=PARAMS,
        cost_estimate=pl.CostEstimate(flops=1 << 16, bytes_accessed=1 << 18, transcendentals=0),
        name="prepare",
    )(hidden, queries)


ORDER = (0, 1, 3, 2)


PART = (OWN_ROWS + 8, HD)
PACKED = (OWN_ROWS + 16, HD)


def store_part(ref, summed, stat):
    ref[:OWN_ROWS, :] = summed
    ref[OWN_ROWS : OWN_ROWS + 1, :] = stat


def pack_part(ref, summed, stat):
    ref[:OWN_ROWS, :] = summed.astype(BF16)
    terms = []
    for _ in range(3):
        terms.append(stat.astype(BF16).astype(F32))
        stat = stat - terms[-1]
    rest = jnp.zeros((PACKED[0] - OWN_ROWS - 3, HD), F32)
    ref[OWN_ROWS:, :] = jnp.concatenate([*terms, rest], axis=0).astype(BF16)


def load_part(ref):
    return ref[:OWN_ROWS, :], ref[OWN_ROWS : OWN_ROWS + 1, :]


def unpack_part(ref):
    stat = jnp.sum(ref[OWN_ROWS:, :].astype(F32), axis=0, keepdims=True)
    return ref[:OWN_ROWS, :].astype(F32), stat


def fetch_kernel(keys_hbm, values_hbm, keys_ref, values_ref, sems):
    copies = (
        pltpu.make_async_copy(keys_hbm, keys_ref, sems.at[0]),
        pltpu.make_async_copy(values_hbm, values_ref, sems.at[1]),
    )
    for copy in copies:
        copy.start()
    for copy in copies:
        copy.wait()


def fetch(keys, values):
    return pl.pallas_call(
        fetch_kernel,
        out_shape=(pltpu.VMEM(keys.shape, BF16), pltpu.VMEM(values.shape, BF16)),
        in_specs=[HBM, HBM],
        out_specs=(VMEM, VMEM),
        scratch_shapes=[pltpu.SemaphoreType.DMA((2,))],
        compiler_params=PARAMS,
        cost_estimate=pl.CostEstimate(flops=1, bytes_accessed=1, transcendentals=0),
        name="fetch",
    )(in_hbm(keys), in_hbm(values))


def attend_kernel(
    lengths_ref,
    near_ref,
    far_ref,
    keys_ref,
    values_ref,
    kept_ref,
    sent_ref,
    spread,
):
    tensor = lax.axis_index("tensor")
    spread[...] = jnp.zeros_like(spread)
    starts = []
    for k in range(TENSOR):
        start = (tensor ^ ORDER[k]) * (LOCAL_HEADS * HD)
        starts.append(start)
        for head in range(LOCAL_HEADS):
            lanes = pl.ds(pl.multiple_of(start + head * HD, HD), HD)
            at = (k % 2) * OWN_ROWS + head * HEAD_ROWS
            to = k * OWN_ROWS + head * HEAD_ROWS
            piece = (near_ref, far_ref)[k // 2][at : at + HEAD_ROWS, :]
            spread[to : to + HEAD_ROWS, lanes] = piece
    scores = lax.dot_general(
        keys_ref[0], spread[...], (((1,), (1,)), ((), ())), preferred_element_type=F32
    ) * (HD**-0.5)
    held = scores.shape[0]
    position = tensor * held + lax.broadcasted_iota(jnp.int32, scores.shape, 0)
    allowed = position < lengths_ref[...]
    masked = jnp.where(allowed, scores, NEG_FILL)
    maxima = jnp.max(masked, axis=0, keepdims=True)
    weights = jnp.where(allowed, jnp.exp(masked - maxima), 0.0)
    totals = jnp.sum(weights, axis=0, keepdims=True)
    rounded = weights.astype(BF16)
    for half, out_ref in enumerate((kept_ref, sent_ref)):
        span = slice(half * 128, half * 128 + 128)
        values = jnp.concatenate(
            [
                values_ref[0, :, pl.ds(pl.multiple_of(starts[2 * half + n], 256), 256)]
                for n in range(2)
            ],
            axis=1,
        )
        summed = lax.dot_general(
            rounded[:, span], values, (((0,), (0,)), ((), ())), preferred_element_type=F32
        )
        low = lane_iota((1, 128)) < OWN_ROWS
        for n in range(2):
            blocks = []
            for head in range(LOCAL_HEADS):
                at = n * LOCAL_HEADS + head
                blocks.append(
                    summed[
                        at * HEAD_ROWS : (at + 1) * HEAD_ROWS, at * HD : (at + 1) * HD
                    ]
                )
            stats = (maxima[:, span], totals[:, span])
            turned = [pltpu.roll(stat, OWN_ROWS, 1) for stat in stats]
            stat = jnp.where(low, *((turned[0], stats[1]) if n else (stats[0], turned[1])))
            if half == 0:
                store_part(kept_ref.at[n], jnp.concatenate(blocks, axis=0), stat)
            else:
                pack_part(sent_ref.at[n], jnp.concatenate(blocks, axis=0), stat)


def attend(lengths, near, far, keys, values):
    return pl.pallas_call(
        attend_kernel,
        out_shape=(
            jax.ShapeDtypeStruct((2, *PART), F32),
            jax.ShapeDtypeStruct((2, *PACKED), BF16),
        ),
        in_specs=[VMEM] * 5,
        out_specs=(VMEM, VMEM),
        scratch_shapes=[pltpu.VMEM((KVH * HEAD_ROWS, KVH * HD), BF16)],
        compiler_params=PARAMS,
        cost_estimate=pl.CostEstimate(flops=1, bytes_accessed=1, transcendentals=0),
        name="attend",
    )(lengths, near, far, keys, values)


def merge_kernel(kept_ref, come_ref, own_ref, next_ref):
    low = lane_iota((1, 128)) < OWN_ROWS
    summed, rows, stats = [], [], []
    for n in range(2):
        parts = (load_part(kept_ref.at[n]), unpack_part(come_ref.at[n]))
        joined = jnp.maximum(parts[0][1], parts[1][1])
        scales = [jnp.exp(stat - joined) for _, stat in parts]
        total = sum(
            stat * pltpu.roll(scale, OWN_ROWS, 1) for (_, stat), scale in zip(parts, scales)
        )
        summed.append([part for part, _ in parts])
        rows += scales
        stats.append(jnp.where(low, joined, total))
    columns = jnp.transpose(jnp.concatenate(rows + rows, axis=0), (1, 0))
    merged = [
        summed[n][0] * columns[:OWN_ROWS, 2 * n : 2 * n + 1]
        + summed[n][1] * columns[:OWN_ROWS, 2 * n + 1 : 2 * n + 2]
        for n in range(2)
    ]
    store_part(own_ref, merged[0], stats[0])
    pack_part(next_ref, merged[1], stats[1])


def merge(kept, come):
    return pl.pallas_call(
        merge_kernel,
        out_shape=(jax.ShapeDtypeStruct(PART, F32), jax.ShapeDtypeStruct(PACKED, BF16)),
        in_specs=[VMEM, VMEM],
        out_specs=(VMEM, VMEM),
        compiler_params=PARAMS,
        cost_estimate=pl.CostEstimate(
            flops=1 << 17, bytes_accessed=1 << 18, transcendentals=1 << 9
        ),
        name="merge",
    )(kept, come)


def project_kernel(hidden_ref, own_ref, other_ref, out_ref, tokens):
    core = lax.axis_index("core")
    x = lax.axis_index("x")
    odd = x % 2 == 1
    for z in range(16):
        tokens[z * STEPS : (z + 1) * STEPS, :] = hidden_ref[z].astype(F32)
    partial = jnp.zeros((16 * STEPS, 512), F32)
    for swap, weight_ref in enumerate((own_ref, other_ref)):
        for pair in range(2):
            at = (core ^ swap) * 256 + ((x // 2) ^ pair) * 128
            block = tokens[:, pl.ds(pl.multiple_of(at, 128), 128)]
            turned = pltpu.roll(block, 64, 1)
            block = jnp.where(odd, *((block, turned) if pair else (turned, block)))
            partial += jnp.dot(
                block.astype(BF16),
                weight_ref[pair * 128 : pair * 128 + 128, :],
                preferred_element_type=F32,
            )
    leading = partial.astype(BF16).astype(F32)
    trailing = (partial - leading)[:, :WIDTH]
    for z in range(16):
        at = TOKENS_ORDER.index(z) * STEPS
        out_ref[SUMS_ORDER.index(z), :, : 2 * WIDTH] = leading[at : at + STEPS, :].astype(BF16)
        out_ref[SUMS_ORDER.index(z), :, 2 * WIDTH :] = trailing[at : at + STEPS, :].astype(BF16)


def project(hidden, own, other):
    return pl.pallas_call(
        project_kernel,
        out_shape=jax.ShapeDtypeStruct((16, STEPS, 3 * WIDTH), BF16),
        in_specs=[VMEM, VMEM, VMEM],
        out_specs=VMEM,
        scratch_shapes=[pltpu.VMEM((64, 512), F32)],
        compiler_params=PARAMS,
        cost_estimate=pl.CostEstimate(
            flops=2 * 64 * 512 * 512, bytes_accessed=1 << 20, transcendentals=0
        ),
        name="project",
    )(hidden, own, other)


def finish_kernel(
    part0_ref,
    part1_ref,
    sums_ref,
    queries_ref,
    cos_ref,
    sin_ref,
    attended_ref,
    keys_ref,
    values_ref,
    wide,
):
    parts = (load_part(part0_ref), unpack_part(part1_ref))
    projected = jnp.sum(sums_ref[...].astype(F32), axis=0)
    new_keys = projected[:, :WIDTH] + projected[:, 2 * WIDTH :]
    cos_part = cos_ref[...]
    sin_part = sin_ref[...]
    new_values = projected[:, WIDTH : 2 * WIDTH].astype(BF16)
    values_ref[...] = new_values
    queries = queries_ref[:OWN_ROWS]
    fresh = []
    for head in range(LOCAL_HEADS):
        front = new_keys[:, head * HD : (head + 1) * HD]
        turned = (front * cos_part + pltpu.roll(front, HD // 2, 1) * sin_part).astype(BF16)
        keys_ref[:, head * HD : (head + 1) * HD] = turned
        fresh.append(
            lax.dot_general(
                turned, queries, (((1,), (1,)), ((), ())), preferred_element_type=F32
            )
        )
    lane = lane_iota((STEPS, OWN_ROWS))
    scores = jnp.where(lane < HEAD_ROWS, fresh[0], fresh[1]) * (HD**-0.5)
    step = (lane % HEAD_ROWS) // GROUP
    allowed = lax.broadcasted_iota(jnp.int32, (STEPS, OWN_ROWS), 0) <= step
    masked = jnp.where(allowed, scores, NEG_FILL)
    maxima = [stat[:, :OWN_ROWS] for _, stat in parts]
    joined = jnp.max(masked, axis=0, keepdims=True)
    for part in maxima:
        joined = jnp.maximum(joined, part)
    weights = jnp.where(allowed, jnp.exp(masked - joined), 0.0)
    totals = jnp.sum(weights, axis=0, keepdims=True)
    scales = []
    for t in range(len(parts)):
        scale = jnp.exp(maxima[t] - joined)
        totals += pltpu.roll(parts[t][1], OWN_ROWS, 1)[:, :OWN_ROWS] * scale
        scales.append(scale)
    factors = jnp.concatenate([*scales, weights.astype(BF16).astype(F32)], axis=0) / totals
    factors = jnp.concatenate([factors, jnp.zeros((6, 128 - OWN_ROWS), F32)], axis=1)
    factors = jnp.concatenate([factors, jnp.zeros((2, 128), F32)], axis=0)
    columns = jnp.transpose(factors, (1, 0))
    values = new_values.astype(F32)
    for head in range(LOCAL_HEADS):
        rows = slice(head * HEAD_ROWS, (head + 1) * HEAD_ROWS)
        total = jnp.zeros((HEAD_ROWS, HD), F32)
        for t in range(len(parts)):
            total += parts[t][0][rows, :] * columns[rows, t : t + 1]
        for t in range(STEPS):
            total += columns[rows, 2 + t : 3 + t] * values[t : t + 1, head * HD : (head + 1) * HD]
        for s in range(STEPS):
            for member in range(GROUP):
                at = (head * GROUP + member) * HD
                row = s * GROUP + member
                wide[s : s + 1, at : at + HD] = total[row : row + 1, :]
    attended_ref[...] = wide[...].astype(BF16)


def finish(parts, sums, queries, cos_part, sin_part):
    return pl.pallas_call(
        finish_kernel,
        out_shape=(
            jax.ShapeDtypeStruct((STEPS, LOCAL_HEADS * GROUP * HD), BF16),
            jax.ShapeDtypeStruct((STEPS, LOCAL_HEADS * HD), BF16),
            jax.ShapeDtypeStruct((STEPS, LOCAL_HEADS * HD), BF16),
        ),
        in_specs=[VMEM] * 6,
        out_specs=(VMEM,) * 3,
        scratch_shapes=[pltpu.VMEM((STEPS, LOCAL_HEADS * GROUP * HD), F32)],
        compiler_params=PARAMS,
        cost_estimate=pl.CostEstimate(
            flops=1 << 20, bytes_accessed=1 << 19, transcendentals=1 << 10
        ),
        name="finish",
    )(*parts, sums, queries, cos_part, sin_part)


def rotation(lengths):
    half = HD // 2
    positions = lengths[None, :] + jnp.arange(STEPS, dtype=jnp.int32)[:, None]
    frequency = ROPE_BASE ** (-jnp.arange(half, dtype=F32) * 2.0 / HD)
    phases = positions.astype(F32) * frequency[None, :]
    cos_part = jnp.cos(phases)
    sin_part = jnp.sin(phases)
    return (
        jnp.concatenate([cos_part, cos_part], axis=-1),
        jnp.concatenate([-sin_part, sin_part], axis=-1),
    )


def exchange_z(blocks, order):
    return lax.all_to_all(blocks, Z_AXES, 0, 0, axis_index_groups=[order])


def with_partner(values, axis, flip, size=4):
    return lax.ppermute(values, axis, [(i, i ^ flip) for i in range(size)])


def body(hidden, kv_weight, queries, key_cache, value_cache, lengths):
    weight = kv_weight.reshape(64, 512)
    chunks, own_queries = prepare(
        gate(hidden.reshape(STEPS, -1), weight), queries.reshape(STEPS, -1)
    )
    come = with_partner(weight, "x", 1)
    weight = jnp.concatenate([weight, come], axis=0)
    near = jnp.concatenate([own_queries, with_partner(own_queries, "tensor", 1)], axis=0)
    tokens = exchange_z(gate(chunks, come), TOKENS_ORDER)
    far = with_partner(near, "tensor", 3)
    weight = jnp.concatenate([weight, with_partner(weight, "x", 3)], axis=0)
    keys, values = fetch(gate(key_cache, weight), value_cache)
    kept, sent = attend(jnp.broadcast_to(lengths, (1, KVH * HEAD_ROWS)), near, far, keys, values)
    other = with_partner(weight, "core", 1, 2)
    partial = project(tokens, weight, gate(other, kept))
    sums = exchange_z(partial, SUMS_ORDER)
    own_part, next_part = merge(kept, with_partner(sent, "tensor", 3))
    parts = (own_part, with_partner(next_part, "tensor", 1))
    cos_part, sin_part = rotation(lengths)
    outs = finish(parts, sums, near, cos_part, sin_part)
    return tuple(out.reshape(STEPS, 1, -1) for out in outs)


def solution(mesh):
    split = Mesh(mesh.devices.reshape(8, 2, 4, 4, 2), ("zlo", "core", "tensor", "x", "zhi"))
    return jax.shard_map(
        body,
        mesh=split,
        in_specs=(
            P(None, ROWS_AXES, None),
            P(ROWS_AXES, None, "tensor"),
            P(None, ROWS_AXES, "tensor"),
            P(ROWS_AXES, "tensor", None),
            P(ROWS_AXES, "tensor", None),
            P(ROWS_AXES),
        ),
        out_specs=(
            P(None, ROWS_AXES, "tensor"),
            P(None, ROWS_AXES, "tensor"),
            P(None, ROWS_AXES, "tensor"),
        ),
        check_vma=False,
    )
```

```python
import jax
import jax.numpy as jnp
from jax import lax
from jax.experimental import pallas as pl
from jax.experimental.pallas import tpu as pltpu
from jax.sharding import Mesh
from jax.sharding import PartitionSpec as P

KVH = 8
HQ = 64
HD = 128
STEPS = 4
GROUP = HQ // KVH
TENSOR = 4
LOCAL_HEADS = KVH // TENSOR
HEAD_ROWS = STEPS * GROUP
OWN_ROWS = LOCAL_HEADS * HEAD_ROWS
WIDTH = LOCAL_HEADS * HD
ROPE_BASE = 500000.0
NEG_FILL = -1e30
F32 = jnp.float32
BF16 = jnp.bfloat16
PARAMS = pltpu.CompilerParams(vmem_limit_bytes=16 * 1024 * 1024)
ROWS_AXES = ("zlo", "core", "x", "zhi")
Z_AXES = ("zhi", "zlo")
def ring(first):
    return [(first + hops) % 16 for hops in range(16)]


TOKENS_ORDER = ring(11)
SUMS_ORDER = ring(0)


def lane_iota(shape):
    return lax.broadcasted_iota(jnp.int32, shape, 1)


SMEM = pl.BlockSpec(memory_space=pltpu.SMEM)
VMEM = pl.BlockSpec(memory_space=pltpu.VMEM)
HBM = pl.BlockSpec(memory_space=pltpu.HBM)


def gate(values, *after):
    return lax.optimization_barrier((values, *after))[0]


def in_hbm(array):
    return pltpu.with_memory_space_constraint(array, pltpu.HBM)


def prepare_kernel(hidden_ref, queries_ref, hidden_out, queries_out, rows):
    for head in range(LOCAL_HEADS):
        for member in range(GROUP):
            at = (head * GROUP + member) * HD
            piece = queries_ref[:, at : at + HD].astype(F32)
            for step in range(STEPS):
                row = head * HEAD_ROWS + step * GROUP + member
                rows[row : row + 1, :] = piece[step : step + 1, :]
    queries_out[...] = rows[...].astype(BF16)
    low = lane_iota((STEPS, 128)) < 64
    for zlo in range(8):
        for pair in range(4):
            at = zlo * 1024 + pair * 256
            one = hidden_ref[:, at : at + 128].astype(F32)
            two = hidden_ref[:, at + 128 : at + 256].astype(F32)
            to = slice(pair * 128, pair * 128 + 128)
            even = jnp.where(low, one, pltpu.roll(two, 64, 1)).astype(BF16)
            odd = jnp.where(low, pltpu.roll(one, 64, 1), two).astype(BF16)
            hidden_out[TOKENS_ORDER.index(zlo), :, to] = even
            hidden_out[TOKENS_ORDER.index(8 + zlo), :, to] = odd


def prepare(hidden, queries):
    return pl.pallas_call(
        prepare_kernel,
        out_shape=(
            jax.ShapeDtypeStruct((16, STEPS, 512), BF16),
            jax.ShapeDtypeStruct((OWN_ROWS, HD), BF16),
        ),
        in_specs=[VMEM, VMEM],
        out_specs=(VMEM, VMEM),
        scratch_shapes=[pltpu.VMEM((OWN_ROWS, HD), F32)],
        compiler_params=PARAMS,
        cost_estimate=pl.CostEstimate(flops=1 << 16, bytes_accessed=1 << 18, transcendentals=0),
        name="prepare",
    )(hidden, queries)


ORDER = (0, 3, 1, 2)


PART = (OWN_ROWS + 8, HD)
PACKED = (OWN_ROWS + 16, HD)


def store_part(ref, summed, stat):
    ref[:OWN_ROWS, :] = summed
    ref[OWN_ROWS : OWN_ROWS + 1, :] = stat


def pack_part(ref, summed, stat):
    ref[:OWN_ROWS, :] = summed.astype(BF16)
    terms = []
    for _ in range(3):
        terms.append(stat.astype(BF16).astype(F32))
        stat = stat - terms[-1]
    rest = jnp.zeros((PACKED[0] - OWN_ROWS - 3, HD), F32)
    ref[OWN_ROWS:, :] = jnp.concatenate([*terms, rest], axis=0).astype(BF16)


def load_part(ref):
    return ref[:OWN_ROWS, :], ref[OWN_ROWS : OWN_ROWS + 1, :]


def unpack_part(ref):
    stat = jnp.sum(ref[OWN_ROWS:, :].astype(F32), axis=0, keepdims=True)
    return ref[:OWN_ROWS, :].astype(F32), stat


def fetch_kernel(keys_hbm, values_hbm, keys_ref, values_ref, sems):
    copies = (
        pltpu.make_async_copy(keys_hbm, keys_ref, sems.at[0]),
        pltpu.make_async_copy(values_hbm, values_ref, sems.at[1]),
    )
    for copy in copies:
        copy.start()
    for copy in copies:
        copy.wait()


def fetch(keys, values):
    return pl.pallas_call(
        fetch_kernel,
        out_shape=(pltpu.VMEM(keys.shape, BF16), pltpu.VMEM(values.shape, BF16)),
        in_specs=[HBM, HBM],
        out_specs=(VMEM, VMEM),
        scratch_shapes=[pltpu.SemaphoreType.DMA((2,))],
        compiler_params=PARAMS,
        cost_estimate=pl.CostEstimate(flops=1, bytes_accessed=1, transcendentals=0),
        name="fetch",
    )(in_hbm(keys), in_hbm(values))


def attend_kernel(
    lengths_ref,
    near_ref,
    far_ref,
    keys_ref,
    values_ref,
    kept_ref,
    sent_ref,
    spread,
):
    tensor = lax.axis_index("tensor")
    spread[...] = jnp.zeros_like(spread)
    starts = []
    for k in range(TENSOR):
        start = (tensor ^ ORDER[k]) * (LOCAL_HEADS * HD)
        starts.append(start)
        for head in range(LOCAL_HEADS):
            lanes = pl.ds(pl.multiple_of(start + head * HD, HD), HD)
            at = (k // 2) * OWN_ROWS + head * HEAD_ROWS
            to = k * OWN_ROWS + head * HEAD_ROWS
            piece = (near_ref, far_ref)[k % 2][at : at + HEAD_ROWS, :]
            spread[to : to + HEAD_ROWS, lanes] = piece
    scores = lax.dot_general(
        keys_ref[0], spread[...], (((1,), (1,)), ((), ())), preferred_element_type=F32
    ) * (HD**-0.5)
    held = scores.shape[0]
    position = tensor * held + lax.broadcasted_iota(jnp.int32, scores.shape, 0)
    allowed = position < lengths_ref[...]
    masked = jnp.where(allowed, scores, NEG_FILL)
    maxima = jnp.max(masked, axis=0, keepdims=True)
    weights = jnp.where(allowed, jnp.exp(masked - maxima), 0.0)
    totals = jnp.sum(weights, axis=0, keepdims=True)
    rounded = weights.astype(BF16)
    for half, out_ref in enumerate((kept_ref, sent_ref)):
        span = slice(half * 128, half * 128 + 128)
        values = jnp.concatenate(
            [
                values_ref[0, :, pl.ds(pl.multiple_of(starts[2 * half + n], 256), 256)]
                for n in range(2)
            ],
            axis=1,
        )
        summed = lax.dot_general(
            rounded[:, span], values, (((0,), (0,)), ((), ())), preferred_element_type=F32
        )
        low = lane_iota((1, 128)) < OWN_ROWS
        for n in range(2):
            blocks = []
            for head in range(LOCAL_HEADS):
                at = n * LOCAL_HEADS + head
                blocks.append(
                    summed[
                        at * HEAD_ROWS : (at + 1) * HEAD_ROWS, at * HD : (at + 1) * HD
                    ]
                )
            stats = (maxima[:, span], totals[:, span])
            turned = [pltpu.roll(stat, OWN_ROWS, 1) for stat in stats]
            stat = jnp.where(low, *((turned[0], stats[1]) if n else (stats[0], turned[1])))
            if half == 0:
                store_part(kept_ref.at[n], jnp.concatenate(blocks, axis=0), stat)
            else:
                pack_part(sent_ref.at[n], jnp.concatenate(blocks, axis=0), stat)


def attend(lengths, near, far, keys, values):
    return pl.pallas_call(
        attend_kernel,
        out_shape=(
            jax.ShapeDtypeStruct((2, *PART), F32),
            jax.ShapeDtypeStruct((2, *PACKED), BF16),
        ),
        in_specs=[VMEM] * 5,
        out_specs=(VMEM, VMEM),
        scratch_shapes=[pltpu.VMEM((KVH * HEAD_ROWS, KVH * HD), BF16)],
        compiler_params=PARAMS,
        cost_estimate=pl.CostEstimate(flops=1, bytes_accessed=1, transcendentals=0),
        name="attend",
    )(lengths, near, far, keys, values)


def merge_kernel(kept_ref, come_ref, own_ref, next_ref):
    low = lane_iota((1, 128)) < OWN_ROWS
    summed, rows, stats = [], [], []
    for n in range(2):
        parts = (load_part(kept_ref.at[n]), unpack_part(come_ref.at[n]))
        joined = jnp.maximum(parts[0][1], parts[1][1])
        scales = [jnp.exp(stat - joined) for _, stat in parts]
        total = sum(
            stat * pltpu.roll(scale, OWN_ROWS, 1) for (_, stat), scale in zip(parts, scales)
        )
        summed.append([part for part, _ in parts])
        rows += scales
        stats.append(jnp.where(low, joined, total))
    columns = jnp.transpose(jnp.concatenate(rows + rows, axis=0), (1, 0))
    merged = [
        summed[n][0] * columns[:OWN_ROWS, 2 * n : 2 * n + 1]
        + summed[n][1] * columns[:OWN_ROWS, 2 * n + 1 : 2 * n + 2]
        for n in range(2)
    ]
    store_part(own_ref, merged[0], stats[0])
    pack_part(next_ref, merged[1], stats[1])


def merge(kept, come):
    return pl.pallas_call(
        merge_kernel,
        out_shape=(jax.ShapeDtypeStruct(PART, F32), jax.ShapeDtypeStruct(PACKED, BF16)),
        in_specs=[VMEM, VMEM],
        out_specs=(VMEM, VMEM),
        compiler_params=PARAMS,
        cost_estimate=pl.CostEstimate(
            flops=1 << 17, bytes_accessed=1 << 18, transcendentals=1 << 9
        ),
        name="merge",
    )(kept, come)


def project_kernel(hidden_ref, own_ref, other_ref, out_ref, tokens):
    core = lax.axis_index("core")
    x = lax.axis_index("x")
    odd = x % 2 == 1
    for z in range(16):
        tokens[z * STEPS : (z + 1) * STEPS, :] = hidden_ref[z].astype(F32)
    partials = []
    for swap, weight_ref in enumerate((own_ref, other_ref)):
        blocks = []
        for pair in range(2):
            at = (core ^ swap) * 256 + ((x // 2) ^ pair) * 128
            block = tokens[:, pl.ds(pl.multiple_of(at, 128), 128)]
            turned = pltpu.roll(block, 64, 1)
            blocks.append(jnp.where(odd, *((block, turned) if pair else (turned, block))))
        partials.append(
            jnp.dot(
                jnp.concatenate(blocks, axis=1).astype(BF16),
                weight_ref[...],
                preferred_element_type=F32,
            )
        )
    partial = partials[0] + partials[1]
    leading = partial.astype(BF16).astype(F32)
    trailing = (partial - leading)[:, :WIDTH]
    for z in range(16):
        at = TOKENS_ORDER.index(z) * STEPS
        out_ref[SUMS_ORDER.index(z), :, : 2 * WIDTH] = leading[at : at + STEPS, :].astype(BF16)
        out_ref[SUMS_ORDER.index(z), :, 2 * WIDTH :] = trailing[at : at + STEPS, :].astype(BF16)


def project(hidden, own, other):
    return pl.pallas_call(
        project_kernel,
        out_shape=jax.ShapeDtypeStruct((16, STEPS, 3 * WIDTH), BF16),
        in_specs=[VMEM, VMEM, VMEM],
        out_specs=VMEM,
        scratch_shapes=[pltpu.VMEM((64, 512), F32)],
        compiler_params=PARAMS,
        cost_estimate=pl.CostEstimate(
            flops=2 * 64 * 512 * 512, bytes_accessed=1 << 20, transcendentals=0
        ),
        name="project",
    )(hidden, own, other)


def finish_kernel(
    part0_ref,
    part1_ref,
    sums_ref,
    queries_ref,
    cos_ref,
    sin_ref,
    attended_ref,
    keys_ref,
    values_ref,
    wide,
):
    parts = (load_part(part0_ref), unpack_part(part1_ref))
    projected = jnp.sum(sums_ref[...].astype(F32), axis=0)
    new_keys = projected[:, :WIDTH] + projected[:, 2 * WIDTH :]
    cos_part = cos_ref[...]
    sin_part = sin_ref[...]
    new_values = projected[:, WIDTH : 2 * WIDTH].astype(BF16)
    values_ref[...] = new_values
    queries = queries_ref[:OWN_ROWS]
    fresh = []
    for head in range(LOCAL_HEADS):
        front = new_keys[:, head * HD : (head + 1) * HD]
        turned = (front * cos_part + pltpu.roll(front, HD // 2, 1) * sin_part).astype(BF16)
        keys_ref[:, head * HD : (head + 1) * HD] = turned
        fresh.append(
            lax.dot_general(
                turned, queries, (((1,), (1,)), ((), ())), preferred_element_type=F32
            )
        )
    lane = lane_iota((STEPS, OWN_ROWS))
    scores = jnp.where(lane < HEAD_ROWS, fresh[0], fresh[1]) * (HD**-0.5)
    step = (lane % HEAD_ROWS) // GROUP
    allowed = lax.broadcasted_iota(jnp.int32, (STEPS, OWN_ROWS), 0) <= step
    masked = jnp.where(allowed, scores, NEG_FILL)
    maxima = [stat[:, :OWN_ROWS] for _, stat in parts]
    joined = jnp.max(masked, axis=0, keepdims=True)
    for part in maxima:
        joined = jnp.maximum(joined, part)
    weights = jnp.where(allowed, jnp.exp(masked - joined), 0.0)
    totals = jnp.sum(weights, axis=0, keepdims=True)
    scales = []
    for t in range(len(parts)):
        scale = jnp.exp(maxima[t] - joined)
        totals += pltpu.roll(parts[t][1], OWN_ROWS, 1)[:, :OWN_ROWS] * scale
        scales.append(scale)
    factors = jnp.concatenate([*scales, weights.astype(BF16).astype(F32)], axis=0) / totals
    factors = jnp.concatenate([factors, jnp.zeros((6, 128 - OWN_ROWS), F32)], axis=1)
    factors = jnp.concatenate([factors, jnp.zeros((2, 128), F32)], axis=0)
    columns = jnp.transpose(factors, (1, 0))
    values = new_values.astype(F32)
    for head in range(LOCAL_HEADS):
        rows = slice(head * HEAD_ROWS, (head + 1) * HEAD_ROWS)
        total = jnp.zeros((HEAD_ROWS, HD), F32)
        for t in range(len(parts)):
            total += parts[t][0][rows, :] * columns[rows, t : t + 1]
        for t in range(STEPS):
            total += columns[rows, 2 + t : 3 + t] * values[t : t + 1, head * HD : (head + 1) * HD]
        for s in range(STEPS):
            for member in range(GROUP):
                at = (head * GROUP + member) * HD
                row = s * GROUP + member
                wide[s : s + 1, at : at + HD] = total[row : row + 1, :]
    attended_ref[...] = wide[...].astype(BF16)


def finish(parts, sums, queries, cos_part, sin_part):
    return pl.pallas_call(
        finish_kernel,
        out_shape=(
            jax.ShapeDtypeStruct((STEPS, LOCAL_HEADS * GROUP * HD), BF16),
            jax.ShapeDtypeStruct((STEPS, LOCAL_HEADS * HD), BF16),
            jax.ShapeDtypeStruct((STEPS, LOCAL_HEADS * HD), BF16),
        ),
        in_specs=[VMEM] * 6,
        out_specs=(VMEM,) * 3,
        scratch_shapes=[pltpu.VMEM((STEPS, LOCAL_HEADS * GROUP * HD), F32)],
        compiler_params=PARAMS,
        cost_estimate=pl.CostEstimate(
            flops=1 << 20, bytes_accessed=1 << 19, transcendentals=1 << 10
        ),
        name="finish",
    )(*parts, sums, queries, cos_part, sin_part)


def rotation(lengths):
    half = HD // 2
    positions = lengths[None, :] + jnp.arange(STEPS, dtype=jnp.int32)[:, None]
    frequency = ROPE_BASE ** (-jnp.arange(half, dtype=F32) * 2.0 / HD)
    phases = positions.astype(F32) * frequency[None, :]
    cos_part = jnp.cos(phases)
    sin_part = jnp.sin(phases)
    return (
        jnp.concatenate([cos_part, cos_part], axis=-1),
        jnp.concatenate([-sin_part, sin_part], axis=-1),
    )


def exchange_z(blocks, order):
    return lax.all_to_all(blocks, Z_AXES, 0, 0, axis_index_groups=[order])


def with_partner(values, axis, flip, size=4):
    return lax.ppermute(values, axis, [(i, i ^ flip) for i in range(size)])


def body(hidden, kv_weight, queries, key_cache, value_cache, lengths):
    weight = kv_weight.reshape(64, 512)
    chunks, own_queries = prepare(
        gate(hidden.reshape(STEPS, -1), weight), queries.reshape(STEPS, -1)
    )
    come = with_partner(weight, "x", 1)
    weight = jnp.concatenate([weight, come], axis=0)
    near = jnp.concatenate([own_queries, with_partner(own_queries, "tensor", 1)], axis=0)
    tokens = exchange_z(gate(chunks, come), TOKENS_ORDER)
    far = with_partner(near, "tensor", 3)
    weight = jnp.concatenate([weight, with_partner(weight, "x", 3)], axis=0)
    keys, values = fetch(gate(key_cache, weight), value_cache)
    kept, sent = attend(jnp.broadcast_to(lengths, (1, KVH * HEAD_ROWS)), near, far, keys, values)
    other = with_partner(weight, "core", 1, 2)
    partial = project(tokens, weight, gate(other, kept))
    sums = exchange_z(partial, SUMS_ORDER)
    own_part, next_part = merge(kept, with_partner(sent, "tensor", 1))
    parts = (own_part, with_partner(next_part, "tensor", 3))
    cos_part, sin_part = rotation(lengths)
    outs = finish(parts, sums, near, cos_part, sin_part)
    return tuple(out.reshape(STEPS, 1, -1) for out in outs)


def solution(mesh):
    split = Mesh(mesh.devices.reshape(8, 2, 4, 4, 2), ("zlo", "core", "tensor", "x", "zhi"))
    return jax.shard_map(
        body,
        mesh=split,
        in_specs=(
            P(None, ROWS_AXES, None),
            P(ROWS_AXES, None, "tensor"),
            P(None, ROWS_AXES, "tensor"),
            P(ROWS_AXES, "tensor", None),
            P(ROWS_AXES, "tensor", None),
            P(ROWS_AXES),
        ),
        out_specs=(
            P(None, ROWS_AXES, "tensor"),
            P(None, ROWS_AXES, "tensor"),
            P(None, ROWS_AXES, "tensor"),
        ),
        check_vma=False,
    )
```

```python
import jax
import jax.numpy as jnp
from jax import lax
from jax.experimental import pallas as pl
from jax.experimental.pallas import tpu as pltpu
from jax.sharding import Mesh
from jax.sharding import PartitionSpec as P

KVH = 8
HQ = 64
HD = 128
STEPS = 4
GROUP = HQ // KVH
TENSOR = 4
LOCAL_HEADS = KVH // TENSOR
HEAD_ROWS = STEPS * GROUP
OWN_ROWS = LOCAL_HEADS * HEAD_ROWS
WIDTH = LOCAL_HEADS * HD
ROPE_BASE = 500000.0
NEG_FILL = -1e30
F32 = jnp.float32
BF16 = jnp.bfloat16
PARAMS = pltpu.CompilerParams(vmem_limit_bytes=16 * 1024 * 1024)
ROWS_AXES = ("zlo", "core", "x", "zhi")
Z_AXES = ("zhi", "zlo")
def ring(first):
    return [(first + hops) % 16 for hops in range(16)]


def outward(first):
    order = [first]
    for hops in range(1, 8):
        order += [(first + hops) % 16, (first - hops) % 16]
    return order + [(first + 8) % 16]


TOKENS_ORDER = ring(11)
SUMS_ORDER = outward(0)


def lane_iota(shape):
    return lax.broadcasted_iota(jnp.int32, shape, 1)


SMEM = pl.BlockSpec(memory_space=pltpu.SMEM)
VMEM = pl.BlockSpec(memory_space=pltpu.VMEM)
HBM = pl.BlockSpec(memory_space=pltpu.HBM)


def gate(values, *after):
    return lax.optimization_barrier((values, *after))[0]


def in_hbm(array):
    return pltpu.with_memory_space_constraint(array, pltpu.HBM)


def prepare_kernel(hidden_ref, queries_ref, hidden_out, queries_out, rows):
    for head in range(LOCAL_HEADS):
        for member in range(GROUP):
            at = (head * GROUP + member) * HD
            piece = queries_ref[:, at : at + HD].astype(F32)
            for step in range(STEPS):
                row = head * HEAD_ROWS + step * GROUP + member
                rows[row : row + 1, :] = piece[step : step + 1, :]
    queries_out[...] = rows[...].astype(BF16)
    low = lane_iota((STEPS, 128)) < 64
    for zlo in range(8):
        for pair in range(4):
            at = zlo * 1024 + pair * 256
            one = hidden_ref[:, at : at + 128].astype(F32)
            two = hidden_ref[:, at + 128 : at + 256].astype(F32)
            to = slice(pair * 128, pair * 128 + 128)
            even = jnp.where(low, one, pltpu.roll(two, 64, 1)).astype(BF16)
            odd = jnp.where(low, pltpu.roll(one, 64, 1), two).astype(BF16)
            hidden_out[TOKENS_ORDER.index(zlo), :, to] = even
            hidden_out[TOKENS_ORDER.index(8 + zlo), :, to] = odd


def prepare(hidden, queries):
    return pl.pallas_call(
        prepare_kernel,
        out_shape=(
            jax.ShapeDtypeStruct((16, STEPS, 512), BF16),
            jax.ShapeDtypeStruct((OWN_ROWS, HD), BF16),
        ),
        in_specs=[VMEM, VMEM],
        out_specs=(VMEM, VMEM),
        scratch_shapes=[pltpu.VMEM((OWN_ROWS, HD), F32)],
        compiler_params=PARAMS,
        cost_estimate=pl.CostEstimate(flops=1 << 16, bytes_accessed=1 << 18, transcendentals=0),
        name="prepare",
    )(hidden, queries)


ORDER = (0, 1, 3, 2)


PART = (OWN_ROWS + 8, HD)
PACKED = (OWN_ROWS + 16, HD)


def store_part(ref, summed, stat):
    ref[:OWN_ROWS, :] = summed
    ref[OWN_ROWS : OWN_ROWS + 1, :] = stat


def pack_part(ref, summed, stat):
    ref[:OWN_ROWS, :] = summed.astype(BF16)
    terms = []
    for _ in range(3):
        terms.append(stat.astype(BF16).astype(F32))
        stat = stat - terms[-1]
    rest = jnp.zeros((PACKED[0] - OWN_ROWS - 3, HD), F32)
    ref[OWN_ROWS:, :] = jnp.concatenate([*terms, rest], axis=0).astype(BF16)


def load_part(ref):
    return ref[:OWN_ROWS, :], ref[OWN_ROWS : OWN_ROWS + 1, :]


def unpack_part(ref):
    stat = jnp.sum(ref[OWN_ROWS:, :].astype(F32), axis=0, keepdims=True)
    return ref[:OWN_ROWS, :].astype(F32), stat


def fetch_kernel(keys_hbm, values_hbm, keys_ref, values_ref, sems):
    copies = (
        pltpu.make_async_copy(keys_hbm, keys_ref, sems.at[0]),
        pltpu.make_async_copy(values_hbm, values_ref, sems.at[1]),
    )
    for copy in copies:
        copy.start()
    for copy in copies:
        copy.wait()


def fetch(keys, values):
    return pl.pallas_call(
        fetch_kernel,
        out_shape=(pltpu.VMEM(keys.shape, BF16), pltpu.VMEM(values.shape, BF16)),
        in_specs=[HBM, HBM],
        out_specs=(VMEM, VMEM),
        scratch_shapes=[pltpu.SemaphoreType.DMA((2,))],
        compiler_params=PARAMS,
        cost_estimate=pl.CostEstimate(flops=1, bytes_accessed=1, transcendentals=0),
        name="fetch",
    )(in_hbm(keys), in_hbm(values))


def attend_kernel(
    lengths_ref,
    near_ref,
    far_ref,
    keys_ref,
    values_ref,
    kept_ref,
    sent_ref,
    spread,
):
    tensor = lax.axis_index("tensor")
    spread[...] = jnp.zeros_like(spread)
    starts = []
    for k in range(TENSOR):
        start = (tensor ^ ORDER[k]) * (LOCAL_HEADS * HD)
        starts.append(start)
        for head in range(LOCAL_HEADS):
            lanes = pl.ds(pl.multiple_of(start + head * HD, HD), HD)
            at = (k % 2) * OWN_ROWS + head * HEAD_ROWS
            to = k * OWN_ROWS + head * HEAD_ROWS
            piece = (near_ref, far_ref)[k // 2][at : at + HEAD_ROWS, :]
            spread[to : to + HEAD_ROWS, lanes] = piece
    scores = lax.dot_general(
        keys_ref[0], spread[...], (((1,), (1,)), ((), ())), preferred_element_type=F32
    ) * (HD**-0.5)
    held = scores.shape[0]
    position = tensor * held + lax.broadcasted_iota(jnp.int32, scores.shape, 0)
    allowed = position < lengths_ref[...]
    masked = jnp.where(allowed, scores, NEG_FILL)
    maxima = jnp.max(masked, axis=0, keepdims=True)
    weights = jnp.where(allowed, jnp.exp(masked - maxima), 0.0)
    totals = jnp.sum(weights, axis=0, keepdims=True)
    rounded = weights.astype(BF16)
    for half, out_ref in enumerate((kept_ref, sent_ref)):
        span = slice(half * 128, half * 128 + 128)
        values = jnp.concatenate(
            [
                values_ref[0, :, pl.ds(pl.multiple_of(starts[2 * half + n], 256), 256)]
                for n in range(2)
            ],
            axis=1,
        )
        summed = lax.dot_general(
            rounded[:, span], values, (((0,), (0,)), ((), ())), preferred_element_type=F32
        )
        low = lane_iota((1, 128)) < OWN_ROWS
        for n in range(2):
            blocks = []
            for head in range(LOCAL_HEADS):
                at = n * LOCAL_HEADS + head
                blocks.append(
                    summed[
                        at * HEAD_ROWS : (at + 1) * HEAD_ROWS, at * HD : (at + 1) * HD
                    ]
                )
            stats = (maxima[:, span], totals[:, span])
            turned = [pltpu.roll(stat, OWN_ROWS, 1) for stat in stats]
            stat = jnp.where(low, *((turned[0], stats[1]) if n else (stats[0], turned[1])))
            if half == 0:
                store_part(kept_ref.at[n], jnp.concatenate(blocks, axis=0), stat)
            else:
                pack_part(sent_ref.at[n], jnp.concatenate(blocks, axis=0), stat)


def attend(lengths, near, far, keys, values):
    return pl.pallas_call(
        attend_kernel,
        out_shape=(
            jax.ShapeDtypeStruct((2, *PART), F32),
            jax.ShapeDtypeStruct((2, *PACKED), BF16),
        ),
        in_specs=[VMEM] * 5,
        out_specs=(VMEM, VMEM),
        scratch_shapes=[pltpu.VMEM((KVH * HEAD_ROWS, KVH * HD), BF16)],
        compiler_params=PARAMS,
        cost_estimate=pl.CostEstimate(flops=1, bytes_accessed=1, transcendentals=0),
        name="attend",
    )(lengths, near, far, keys, values)


def merge_kernel(kept_ref, come_ref, own_ref, next_ref):
    low = lane_iota((1, 128)) < OWN_ROWS
    summed, rows, stats = [], [], []
    for n in range(2):
        parts = (load_part(kept_ref.at[n]), unpack_part(come_ref.at[n]))
        joined = jnp.maximum(parts[0][1], parts[1][1])
        scales = [jnp.exp(stat - joined) for _, stat in parts]
        total = sum(
            stat * pltpu.roll(scale, OWN_ROWS, 1) for (_, stat), scale in zip(parts, scales)
        )
        summed.append([part for part, _ in parts])
        rows += scales
        stats.append(jnp.where(low, joined, total))
    columns = jnp.transpose(jnp.concatenate(rows + rows, axis=0), (1, 0))
    merged = [
        summed[n][0] * columns[:OWN_ROWS, 2 * n : 2 * n + 1]
        + summed[n][1] * columns[:OWN_ROWS, 2 * n + 1 : 2 * n + 2]
        for n in range(2)
    ]
    store_part(own_ref, merged[0], stats[0])
    pack_part(next_ref, merged[1], stats[1])


def merge(kept, come):
    return pl.pallas_call(
        merge_kernel,
        out_shape=(jax.ShapeDtypeStruct(PART, F32), jax.ShapeDtypeStruct(PACKED, BF16)),
        in_specs=[VMEM, VMEM],
        out_specs=(VMEM, VMEM),
        compiler_params=PARAMS,
        cost_estimate=pl.CostEstimate(
            flops=1 << 17, bytes_accessed=1 << 18, transcendentals=1 << 9
        ),
        name="merge",
    )(kept, come)


def project_kernel(hidden_ref, own_ref, other_ref, out_ref, tokens):
    core = lax.axis_index("core")
    x = lax.axis_index("x")
    odd = x % 2 == 1
    for z in range(16):
        tokens[z * STEPS : (z + 1) * STEPS, :] = hidden_ref[z].astype(F32)
    partial = jnp.zeros((16 * STEPS, 512), F32)
    for swap, weight_ref in enumerate((own_ref, other_ref)):
        for pair in range(2):
            at = (core ^ swap) * 256 + ((x // 2) ^ pair) * 128
            block = tokens[:, pl.ds(pl.multiple_of(at, 128), 128)]
            turned = pltpu.roll(block, 64, 1)
            block = jnp.where(odd, *((block, turned) if pair else (turned, block)))
            partial += jnp.dot(
                block.astype(BF16),
                weight_ref[pair * 128 : pair * 128 + 128, :],
                preferred_element_type=F32,
            )
    leading = partial.astype(BF16).astype(F32)
    trailing = (partial - leading)[:, :WIDTH]
    for z in range(16):
        at = TOKENS_ORDER.index(z) * STEPS
        out_ref[SUMS_ORDER.index(z), :, : 2 * WIDTH] = leading[at : at + STEPS, :].astype(BF16)
        out_ref[SUMS_ORDER.index(z), :, 2 * WIDTH :] = trailing[at : at + STEPS, :].astype(BF16)


def project(hidden, own, other):
    return pl.pallas_call(
        project_kernel,
        out_shape=jax.ShapeDtypeStruct((16, STEPS, 3 * WIDTH), BF16),
        in_specs=[VMEM, VMEM, VMEM],
        out_specs=VMEM,
        scratch_shapes=[pltpu.VMEM((64, 512), F32)],
        compiler_params=PARAMS,
        cost_estimate=pl.CostEstimate(
            flops=2 * 64 * 512 * 512, bytes_accessed=1 << 20, transcendentals=0
        ),
        name="project",
    )(hidden, own, other)


def finish_kernel(
    part0_ref,
    part1_ref,
    sums_ref,
    queries_ref,
    cos_ref,
    sin_ref,
    attended_ref,
    keys_ref,
    values_ref,
    wide,
):
    parts = (load_part(part0_ref), unpack_part(part1_ref))
    projected = jnp.sum(sums_ref[...].astype(F32), axis=0)
    new_keys = projected[:, :WIDTH] + projected[:, 2 * WIDTH :]
    cos_part = cos_ref[...]
    sin_part = sin_ref[...]
    new_values = projected[:, WIDTH : 2 * WIDTH].astype(BF16)
    values_ref[...] = new_values
    queries = queries_ref[:OWN_ROWS]
    fresh = []
    for head in range(LOCAL_HEADS):
        front = new_keys[:, head * HD : (head + 1) * HD]
        turned = (front * cos_part + pltpu.roll(front, HD // 2, 1) * sin_part).astype(BF16)
        keys_ref[:, head * HD : (head + 1) * HD] = turned
        fresh.append(
            lax.dot_general(
                turned, queries, (((1,), (1,)), ((), ())), preferred_element_type=F32
            )
        )
    lane = lane_iota((STEPS, OWN_ROWS))
    scores = jnp.where(lane < HEAD_ROWS, fresh[0], fresh[1]) * (HD**-0.5)
    step = (lane % HEAD_ROWS) // GROUP
    allowed = lax.broadcasted_iota(jnp.int32, (STEPS, OWN_ROWS), 0) <= step
    masked = jnp.where(allowed, scores, NEG_FILL)
    maxima = [stat[:, :OWN_ROWS] for _, stat in parts]
    joined = jnp.max(masked, axis=0, keepdims=True)
    for part in maxima:
        joined = jnp.maximum(joined, part)
    weights = jnp.where(allowed, jnp.exp(masked - joined), 0.0)
    totals = jnp.sum(weights, axis=0, keepdims=True)
    scales = []
    for t in range(len(parts)):
        scale = jnp.exp(maxima[t] - joined)
        totals += pltpu.roll(parts[t][1], OWN_ROWS, 1)[:, :OWN_ROWS] * scale
        scales.append(scale)
    factors = jnp.concatenate([*scales, weights.astype(BF16).astype(F32)], axis=0) / totals
    factors = jnp.concatenate([factors, jnp.zeros((6, 128 - OWN_ROWS), F32)], axis=1)
    factors = jnp.concatenate([factors, jnp.zeros((2, 128), F32)], axis=0)
    columns = jnp.transpose(factors, (1, 0))
    values = new_values.astype(F32)
    for head in range(LOCAL_HEADS):
        rows = slice(head * HEAD_ROWS, (head + 1) * HEAD_ROWS)
        total = jnp.zeros((HEAD_ROWS, HD), F32)
        for t in range(len(parts)):
            total += parts[t][0][rows, :] * columns[rows, t : t + 1]
        for t in range(STEPS):
            total += columns[rows, 2 + t : 3 + t] * values[t : t + 1, head * HD : (head + 1) * HD]
        for s in range(STEPS):
            for member in range(GROUP):
                at = (head * GROUP + member) * HD
                row = s * GROUP + member
                wide[s : s + 1, at : at + HD] = total[row : row + 1, :]
    attended_ref[...] = wide[...].astype(BF16)


def finish(parts, sums, queries, cos_part, sin_part):
    return pl.pallas_call(
        finish_kernel,
        out_shape=(
            jax.ShapeDtypeStruct((STEPS, LOCAL_HEADS * GROUP * HD), BF16),
            jax.ShapeDtypeStruct((STEPS, LOCAL_HEADS * HD), BF16),
            jax.ShapeDtypeStruct((STEPS, LOCAL_HEADS * HD), BF16),
        ),
        in_specs=[VMEM] * 6,
        out_specs=(VMEM,) * 3,
        scratch_shapes=[pltpu.VMEM((STEPS, LOCAL_HEADS * GROUP * HD), F32)],
        compiler_params=PARAMS,
        cost_estimate=pl.CostEstimate(
            flops=1 << 20, bytes_accessed=1 << 19, transcendentals=1 << 10
        ),
        name="finish",
    )(*parts, sums, queries, cos_part, sin_part)


def rotation(lengths):
    half = HD // 2
    positions = lengths[None, :] + jnp.arange(STEPS, dtype=jnp.int32)[:, None]
    frequency = ROPE_BASE ** (-jnp.arange(half, dtype=F32) * 2.0 / HD)
    phases = positions.astype(F32) * frequency[None, :]
    cos_part = jnp.cos(phases)
    sin_part = jnp.sin(phases)
    return (
        jnp.concatenate([cos_part, cos_part], axis=-1),
        jnp.concatenate([-sin_part, sin_part], axis=-1),
    )


def exchange_z(blocks, order):
    return lax.all_to_all(blocks, Z_AXES, 0, 0, axis_index_groups=[order])


def with_partner(values, axis, flip, size=4):
    return lax.ppermute(values, axis, [(i, i ^ flip) for i in range(size)])


def body(hidden, kv_weight, queries, key_cache, value_cache, lengths):
    weight = kv_weight.reshape(64, 512)
    chunks, own_queries = prepare(
        gate(hidden.reshape(STEPS, -1), weight), queries.reshape(STEPS, -1)
    )
    come = with_partner(weight, "x", 1)
    weight = jnp.concatenate([weight, come], axis=0)
    near = jnp.concatenate([own_queries, with_partner(own_queries, "tensor", 1)], axis=0)
    tokens = exchange_z(gate(chunks, come), TOKENS_ORDER)
    far = with_partner(near, "tensor", 3)
    weight = jnp.concatenate([weight, with_partner(weight, "x", 3)], axis=0)
    keys, values = fetch(gate(key_cache, weight), value_cache)
    kept, sent = attend(jnp.broadcast_to(lengths, (1, KVH * HEAD_ROWS)), near, far, keys, values)
    other = with_partner(weight, "core", 1, 2)
    partial = project(tokens, weight, gate(other, kept))
    sums = exchange_z(partial, SUMS_ORDER)
    own_part, next_part = merge(kept, with_partner(sent, "tensor", 3))
    parts = (own_part, with_partner(next_part, "tensor", 1))
    cos_part, sin_part = rotation(lengths)
    outs = finish(parts, sums, near, cos_part, sin_part)
    return tuple(out.reshape(STEPS, 1, -1) for out in outs)


def solution(mesh):
    split = Mesh(mesh.devices.reshape(8, 2, 4, 4, 2), ("zlo", "core", "tensor", "x", "zhi"))
    return jax.shard_map(
        body,
        mesh=split,
        in_specs=(
            P(None, ROWS_AXES, None),
            P(ROWS_AXES, None, "tensor"),
            P(None, ROWS_AXES, "tensor"),
            P(ROWS_AXES, "tensor", None),
            P(ROWS_AXES, "tensor", None),
            P(ROWS_AXES),
        ),
        out_specs=(
            P(None, ROWS_AXES, "tensor"),
            P(None, ROWS_AXES, "tensor"),
            P(None, ROWS_AXES, "tensor"),
        ),
        check_vma=False,
    )
```
